512 devices in a mesh: ctx: 32 (over x, z), heads: 8 (over y), dp: 2 (over core).
Axes of the slice: x: 4, y: 8, z: 8, core: 2. Of those that a mesh axis runs over, the one named last changes fastest.
Arguments:
- queries: bfloat16 [2, 8192, 8192], P('dp', 'ctx', 'heads'), may hold values from -6 to 6
- keys: bfloat16 [2, 8192, 8192], P('dp', 'ctx', 'heads'), may hold values from -6 to 6
- values: bfloat16 [2, 8192, 8192], P('dp', 'ctx', 'heads'), may hold values from -76 to 76, as said below
- gain: float32 [8192], P('heads'), may hold values from 0.1 to 1.9
- grad_out: bfloat16 [2, 8192, 8192], P('dp', 'ctx', 'heads'), may hold values from -6 to 6
Outputs:
- output: bfloat16 [2, 8192, 8192], P('dp', 'ctx', 'heads')
- grad_queries: bfloat16 [2, 8192, 8192], P('dp', 'ctx', 'heads')
- grad_keys: bfloat16 [2, 8192, 8192], P('dp', 'ctx', 'heads')
- grad_values: bfloat16 [2, 8192, 8192], P('dp', 'ctx', 'heads')
- grad_gain: float32 [8192], P('heads')
The draws below stay inside these ranges and needn't reach their ends.
Inputs may be any that keep to these rules, and one draw needn't show every extreme that they name: The values' columns are scaled so that their size grows about threefold from the first head to the last, with further random scales per column and per token.
All inputs are finite; a program needn't handle non-finite values.
Results may differ from the reference program's by a relative error of at most 0.0012.
Values sent between devices are 32-bit elements; how exact they have to be, the bound alone decides.
No kernel may reach another device: no remote copies, remote signals or barrier semaphores. Data moves between devices by JAX's collectives and lax.ppermute only.
A program may use at most 128 MiB of HBM per device.

```python
import jax
import jax.numpy as jnp
from jax import lax

H = 64
DH = 128
SEQ = 8192
BATCH = 2


def draw_values(key, part):
    key = jax.random.fold_in(key, 7)
    base_key, column_key, row_key = jax.random.split(key, 3)
    shape = (BATCH, SEQ, H * DH)
    column = (jnp.arange(H * DH) // DH).astype(jnp.float32)
    trend = 3.0 ** (column / max(H - 1, 1))
    column_scale = trend * 10.0 ** (0.5 * jax.random.uniform(column_key, (H * DH,), jnp.float32))
    row_scale = 10.0 ** (0.3 * jax.random.uniform(row_key, (BATCH, SEQ, 1), jnp.float32))
    base = jnp.clip(jax.random.normal(base_key, shape, jnp.float32), -4.0, 4.0)
    return (base * column_scale * row_scale).astype(jnp.bfloat16)


def block_scale(own_key, dims, cuts, smallest, largest):
    def one(position, shards_of):
        draws = jax.random.uniform(jax.random.fold_in(jax.random.fold_in(own_key, 6), position), (shards_of,), jnp.float32, smallest / len(cuts), largest / len(cuts))
        return jnp.repeat(jnp.exp(draws), dims[position] // shards_of).reshape((-1,) + (1,) * (len(dims) - position - 1))

    loudness = one(*cuts[0])
    for cut in cuts[1:]:
        loudness = loudness * one(*cut)
    return loudness


def centred(rng, shape, scale, reach, cuts=(), held_as=jnp.bfloat16):
    result = scale * jax.random.normal(rng, shape, jnp.float32)
    if cuts:
        result = result * block_scale(rng, shape, cuts, -0.22, 0.18)
    return jnp.clip(result, -reach, reach).astype(held_as)


def setup_inputs(seed: int = 0) -> dict:
    key_of = jax.random.split(jax.random.key(seed), 6)
    queries = centred(key_of[0], (BATCH, SEQ, H * DH), 1.0, 6.0, ((0, 2), (1, 32), (2, 8)))
    keys = centred(key_of[1], (BATCH, SEQ, H * DH), 1.0, 6.0, ((0, 2), (1, 32), (2, 8)))
    values = draw_values(jax.random.fold_in(key_of[5], 71), 0)
    gain = jnp.clip(1.0 + 0.18 * jax.random.normal(key_of[3], (H * DH,), jnp.float32), 0.1, 1.9)
    grad_out = centred(key_of[4], (BATCH, SEQ, H * DH), 1.0, 6.0, ((0, 2), (1, 32), (2, 8)))
    return {"queries": queries, "keys": keys, "values": values, "gain": gain, "grad_out": grad_out}


epsilon = 1e-05

def attend(query_head, key_head, value_head):
    seq = query_head.shape[0]
    rows = min(512, seq)
    count = seq // rows
    mask = jnp.tril(jnp.ones((rows, rows), jnp.float32))
    scaled = (query_head * DH ** (-0.5)).reshape(count, rows, DH)
    key_blocks = key_head.reshape(count, rows, DH)
    value_blocks = value_head.reshape(count, rows, DH)

    def advance(state, item):
        q_block, k_block, v_block = item
        scores = jnp.dot(q_block, k_block.T, precision=lax.Precision.HIGHEST) * mask
        out = jnp.dot(scores, v_block, precision=lax.Precision.HIGHEST)
        out = out + jnp.dot(q_block, state, precision=lax.Precision.HIGHEST)
        state = state + jnp.dot(k_block.T, v_block, precision=lax.Precision.HIGHEST)
        return (state, out)
    start = jnp.zeros((DH, DH), jnp.float32)
    _, outs = lax.scan(advance, start, (scaled, key_blocks, value_blocks))
    return outs.reshape(seq, DH)

def split_heads(array):
    return array.reshape(BATCH, SEQ, H, DH).transpose(0, 2, 1, 3).reshape(BATCH * H, SEQ, DH)

def join_heads(array):
    return array.reshape(BATCH, H, SEQ, DH).transpose(0, 2, 1, 3).reshape(BATCH, SEQ, H * DH)

def normed(attn, gain):
    root = jnp.sqrt(lax.optimization_barrier(jnp.mean(attn * attn, axis=-1, keepdims=True)) + epsilon)
    return gain * attn / root

def reference(queries, keys, values, gain, grad_out):
    q_heads = split_heads(queries.astype(jnp.float32))
    k_heads = split_heads(keys.astype(jnp.float32))
    v_heads = split_heads(values.astype(jnp.float32))
    heads_out = lax.map(lambda item: attend(item[0], item[1], item[2]), (q_heads, k_heads, v_heads))
    attn = join_heads(heads_out)
    output, pull = jax.vjp(normed, attn, gain)
    d_attn, d_gain = pull(grad_out.astype(jnp.float32))
    grad_gain = d_gain / jnp.sqrt(jnp.float32(BATCH * SEQ))
    d_heads = split_heads(d_attn)

    def backward(item):
        q_head, k_head, v_head, d_head = item
        _, pull_head = jax.vjp(attend, q_head, k_head, v_head)
        return pull_head(d_head)
    dq, dk, dv = lax.map(backward, (q_heads, k_heads, v_heads, d_heads))
    return (output.astype(jnp.bfloat16), join_heads(dq).astype(jnp.bfloat16), join_heads(dk).astype(jnp.bfloat16), join_heads(dv).astype(jnp.bfloat16), grad_gain)
```

```python
import functools
import math

import jax
import jax.numpy as jnp
from jax import lax
from jax.experimental import pallas as pl
from jax.experimental.pallas import tpu as pltpu
from jax.sharding import PartitionSpec as P

DH = 128
epsilon = 1e-05
STEP = 2
F32 = jnp.float32
BF16 = jnp.bfloat16


def halves(x):
    upper = x.astype(BF16)
    return upper, (x - upper.astype(F32)).astype(BF16)


def dot(a, b, ca=1, cb=0):
    return lax.dot_general(a, b, (((ca,), (cb,)), ((), ())), preferred_element_type=F32)


def exact_dot(a, b, ca, cb):
    return lax.dot_general(
        a, b, (((ca,), (cb,)), ((), ())), preferred_element_type=F32, precision=lax.Precision.HIGHEST
    )


def columns(head):
    return slice(head * DH, (head + 1) * DH)


def causal(x):
    row = lax.broadcasted_iota(jnp.int32, x.shape, 0)
    column = lax.broadcasted_iota(jnp.int32, x.shape, 1)
    return jnp.where(row >= column, x, 0.0)


def call(kernel, name, grid, ins, outs, flops, arrays):
    moved = sum(a.size * a.dtype.itemsize for a in arrays)
    moved += sum(math.prod(shape) * jnp.dtype(kind).itemsize for _, _, shape, kind in outs)
    return pl.pallas_call(
        kernel,
        name=name,
        grid=grid,
        in_specs=[pl.BlockSpec(block, index) for block, index in ins],
        out_specs=[pl.BlockSpec(block, index) for block, index, _, _ in outs],
        out_shape=[jax.ShapeDtypeStruct(shape, kind) for _, _, shape, kind in outs],
        cost_estimate=pl.CostEstimate(flops=flops, bytes_accessed=moved, transcendentals=0),
        compiler_params=pltpu.CompilerParams(vmem_limit_bytes=48 * 1024 * 1024),
    )(*arrays)


def states_kernel(k_ref, v_ref, state_ref):
    for i in range(STEP):
        at = columns(i)
        state_ref[at, :] = dot(k_ref[:, at], v_ref[:, at], 0, 0)


def inner_kernel(q_ref, k_ref, v_ref, out_ref):
    for i in range(STEP):
        at = columns(i)
        scores = causal(dot(q_ref[:, at], k_ref[:, at], 1, 1))
        upper, lower = halves(scores)
        v = v_ref[:, at]
        out_ref[:, at] = dot(upper, v) + dot(lower, v)


def scan_kernel(reverse, part_ref, out_ref):
    count = part_ref.shape[0]
    total = jnp.zeros(out_ref.shape[1:], F32)
    for i in range(count):
        place = count - 1 - i if reverse else i
        out_ref[place] = total
        total = total + part_ref[place]


def suffix_kernel(rows, part_ref, out_ref, gain_ref):
    count = part_ref.shape[0]
    total = jnp.zeros(out_ref.shape[1:], F32)
    gain = jnp.zeros(gain_ref.shape, F32)
    for i in range(count):
        place = count - 1 - i
        out_ref[place] = total
        total = total + part_ref[place, :rows]
        gain = gain + part_ref[place, rows:]
    gain_ref[...] = gain


def attend_kernel(steps, scale, q_ref, within_ref, state_ref, gain_ref, dy_ref, attn_ref, sums_ref, square_sum, inner_sum):
    step = pl.program_id(0)
    squares = jnp.zeros(square_sum.shape, F32)
    inner = jnp.zeros(inner_sum.shape, F32)
    for i in range(STEP):
        at = columns(i)
        q = q_ref[:, at]
        upper, lower = halves(state_ref[at, :])
        attn = scale * (
            within_ref[:, at]
            + dot(jnp.concatenate([q, q], 1), jnp.concatenate([upper, lower], 0))
        )
        attn_ref[:, at] = attn
        squares += attn * attn
        inner += (gain_ref[:, at] * dy_ref[:, at].astype(F32)) * attn

    @pl.when(step == 0)
    def _():
        square_sum[...] = squares
        inner_sum[...] = inner

    @pl.when(step > 0)
    def _():
        square_sum[...] += squares
        inner_sum[...] += inner

    @pl.when(step == steps - 1)
    def _():
        row = lax.broadcasted_iota(jnp.int32, (8, DH), 0)
        sums = exact_dot(jnp.where(row == 0, 1.0, 0.0), square_sum[...], 1, 1)
        sums += exact_dot(jnp.where(row == 1, 1.0, 0.0), inner_sum[...], 1, 1)
        for i in range(sums_ref.shape[0]):
            sums_ref[i] = sums


def token_factors(sums, width):
    row = lax.broadcasted_iota(jnp.int32, (sums.shape[0], DH), 0) % 8
    squares = exact_dot(sums, jnp.where(row == 0, 1.0, 0.0), 0, 0)
    inner = exact_dot(sums, jnp.where(row == 1, 1.0, 0.0), 0, 0)
    inverse = 1.0 / jnp.sqrt(squares / width + epsilon)
    return inverse, inner * (inverse * inverse * inverse) / width


def grad_state_kernel(width, sums_ref, q_ref, attn_ref, gain_ref, dy_ref, state_ref, factor_ref):
    inverse, other = token_factors(sums_ref[...], width)
    factor_ref[0] = inverse
    factor_ref[1] = other
    heads = q_ref.shape[1] // DH
    per_head = state_ref.shape[0] // heads
    rows = DH // per_head
    weights = []
    for i in range(heads):
        at = columns(i)
        dy = dy_ref[:, at].astype(F32)
        attn = attn_ref[:, at]
        weights.append(jnp.sum(dy * (attn * inverse), axis=0, keepdims=True))
        d_attn = (gain_ref[:, at] * dy) * inverse - attn * other
        upper, lower = halves(d_attn)
        q = q_ref[:, at]
        state = dot(q, upper, 0, 0) + dot(q, lower, 0, 0)
        state_ref[i * per_head : (i + 1) * per_head, :rows, :] = state.reshape(per_head, rows, DH)
    weights = jnp.concatenate(weights, 0)
    for i in range(state_ref.shape[0]):
        state_ref[i, rows:, :] = weights


def backward_kernel(scale, q_ref, k_ref, v_ref, dy_ref, gain_ref, attn_ref, state_ref, factor_ref, out_ref, dq_ref, dk_ref, dv_ref):
    inverse = factor_ref[0]
    other = factor_ref[1]
    for i in range(STEP):
        at = columns(i)
        q, k, v = q_ref[:, at], k_ref[:, at], v_ref[:, at]
        gain = gain_ref[:, at]
        attn = attn_ref[:, at]
        unit = attn * inverse
        out_ref[:, at] = (gain * unit).astype(out_ref.dtype)
        d_attn = (gain * dy_ref[:, at].astype(F32)) * inverse - attn * other
        d_upper, d_lower = halves(d_attn)
        scores = causal(dot(q, k, 1, 1))
        s_upper, s_lower = halves(scores)
        d_scores = causal(
            dot(jnp.concatenate([d_upper, d_lower], 1), jnp.concatenate([v, v], 1), 1, 1)
        )
        ds_upper, ds_lower = halves(d_scores)
        p_upper, p_lower = halves(state_ref[at, :])
        dq = dot(ds_upper, k) + dot(ds_lower, k)
        dq += dot(jnp.concatenate([d_upper, d_lower], 1), jnp.concatenate([p_upper, p_upper], 1), 1, 1)
        dq += dot(d_upper, p_lower, 1, 1)
        dq_ref[:, at] = (scale * dq).astype(dq_ref.dtype)
        dk_ref[:, at] = dot(ds_upper, q, 0, 0) + dot(ds_lower, q, 0, 0)
        dv_ref[:, at] = dot(s_upper, d_upper, 0, 0) + dot(s_upper, d_lower, 0, 0) + dot(s_lower, d_upper, 0, 0)


def last_kernel(scale, k_ref, v_ref, state_ref, dk_in, dv_in, dk_ref, dv_ref):
    for i in range(STEP):
        at = columns(i)
        k, v = k_ref[:, at], v_ref[:, at]
        upper, lower = halves(state_ref[at, :])
        dk = dk_in[:, at] + dot(jnp.concatenate([v, v], 1), jnp.concatenate([upper, lower], 1), 1, 1)
        dv = dv_in[:, at] + dot(jnp.concatenate([k, k], 1), jnp.concatenate([upper, lower], 0))
        dk_ref[:, at] = (scale * dk).astype(dk_ref.dtype)
        dv_ref[:, at] = (scale * dv).astype(dv_ref.dtype)


def body(queries, keys, values, gain, grad_out):
    _, tokens, wide = queries.shape
    q, k, v, dy = (a.reshape(tokens, wide) for a in (queries, keys, values, grad_out))
    gain = gain.reshape(1, wide)
    heads = wide // DH
    ctx, shards = lax.axis_size("ctx"), lax.axis_size("heads")
    width = float(shards * wide)
    scale = DH ** (-0.5)
    steps = heads // STEP
    rows = wide // ctx
    cols = STEP * DH
    per = 2 * tokens * DH * DH * heads

    tok = ((tokens, cols), lambda i: (0, i))
    state = ((cols, DH), lambda i: (i, 0))
    vec = ((1, cols), lambda i: (0, i))
    all_tok = (tokens, wide)

    def whole(*shape):
        return (shape, lambda i: (0,) * len(shape))

    (local,) = call(
        states_kernel, "key_value_states", (steps,), [tok, tok], [(*state, (wide, DH), F32)], per, [k, v]
    )
    parts = lax.all_to_all(local, "ctx", 0, 0, tiled=True)
    (within,) = call(
        inner_kernel, "within_block", (steps,), [tok] * 3, [(*tok, all_tok, F32)], 6 * per, [q, k, v]
    )
    (before,) = call(
        functools.partial(scan_kernel, False),
        "prefix",
        (1,),
        [whole(ctx, rows, DH)],
        [(*whole(ctx, rows, DH), (ctx, rows, DH), F32)],
        wide * DH,
        [parts.reshape(ctx, rows, DH)],
    )
    prefix = lax.all_to_all(before.reshape(wide, DH), "ctx", 0, 0, tiled=True)

    moved = sum(a.size * a.dtype.itemsize for a in (q, within, prefix, dy)) + within.size * 4
    attn, sums = pl.pallas_call(
        functools.partial(attend_kernel, steps, scale),
        name="attend",
        grid=(steps,),
        in_specs=[pl.BlockSpec(*s) for s in (tok, tok, state, vec, tok)],
        out_specs=[pl.BlockSpec(*tok), pl.BlockSpec(*whole(shards, 8, tokens))],
        out_shape=[
            jax.ShapeDtypeStruct(all_tok, F32),
            jax.ShapeDtypeStruct((shards, 8, tokens), F32),
        ],
        scratch_shapes=[pltpu.VMEM((tokens, DH), F32)] * 2,
        cost_estimate=pl.CostEstimate(flops=2 * per, bytes_accessed=moved, transcendentals=0),
        compiler_params=pltpu.CompilerParams(vmem_limit_bytes=48 * 1024 * 1024),
    )(q, within, prefix, gain, dy)
    sums = lax.all_to_all(sums, "heads", 0, 0, tiled=True).reshape(shards * 8, tokens)

    grad_local, factors = call(
        functools.partial(grad_state_kernel, width),
        "grad_states",
        (1,),
        [whole(shards * 8, tokens), whole(*all_tok), whole(*all_tok), whole(1, wide), whole(*all_tok)],
        [
            (*whole(ctx, rows + heads, DH), (ctx, rows + heads, DH), F32),
            (*whole(2, tokens, DH), (2, tokens, DH), F32),
        ],
        2 * per,
        [sums, q, attn, gain, dy],
    )
    grad_parts = lax.all_to_all(grad_local, "ctx", 0, 0, tiled=True)
    output, d_query, dk_part, dv_part = call(
        functools.partial(backward_kernel, scale),
        "backward_within",
        (steps,),
        [tok, tok, tok, tok, vec, tok, state, whole(2, tokens, DH)],
        [(*tok, all_tok, BF16), (*tok, all_tok, BF16), (*tok, all_tok, F32), (*tok, all_tok, F32)],
        22 * per,
        [q, k, v, dy, gain, attn, prefix, factors],
    )
    after, gain_sum = call(
        functools.partial(suffix_kernel, rows),
        "suffix",
        (1,),
        [whole(ctx, rows + heads, DH)],
        [(*whole(ctx, rows, DH), (ctx, rows, DH), F32), (*whole(heads, DH), (heads, DH), F32)],
        wide * DH,
        [grad_parts],
    )
    suffix = lax.all_to_all(after.reshape(wide, DH), "ctx", 0, 0, tiled=True)
    total_rows = lax.axis_size("dp") * ctx * tokens
    grad_gain = lax.psum(gain_sum, "dp").reshape(wide) / math.sqrt(total_rows)
    d_key, d_value = call(
        functools.partial(last_kernel, scale),
        "key_value_gradients",
        (steps,),
        [tok, tok, state, tok, tok],
        [(*tok, all_tok, BF16), (*tok, all_tok, BF16)],
        4 * per,
        [k, v, suffix, dk_part, dv_part],
    )
    return (*(a[None] for a in (output, d_query, d_key, d_value)), grad_gain)


def solution(mesh):
    placed = P("dp", "ctx", "heads")
    return jax.shard_map(
        body,
        mesh=mesh,
        in_specs=(placed, placed, placed, P("heads"), placed),
        out_specs=(placed, placed, placed, placed, P("heads")),
        check_vma=False,
    )
```

```python
import functools
import math

import jax
import jax.numpy as jnp
from jax import lax
from jax.experimental import pallas as pl
from jax.experimental.pallas import tpu as pltpu
from jax.sharding import PartitionSpec as P

DH = 128
epsilon = 1e-05
F32 = jnp.float32
BF16 = jnp.bfloat16
VMEM_GRANT = 16 * 1024 * 1024
SUFFIX_OUT = "hbm"


def halves(x):
    upper = x.astype(BF16)
    return upper, (x - upper.astype(F32)).astype(BF16)


def dot(a, b, ca=1, cb=0):
    return lax.dot_general(a, b, (((ca,), (cb,)), ((), ())), preferred_element_type=F32)


def columns(head):
    return slice(head * DH, (head + 1) * DH)


def causal(x):
    row = lax.broadcasted_iota(jnp.int32, x.shape, 0)
    column = lax.broadcasted_iota(jnp.int32, x.shape, 1)
    return jnp.where(row >= column, x, 0.0)


def call(kernel, name, ins, outs, flops, scratch=(), aliases=None):
    spaces = {"vmem": pltpu.VMEM, "hbm": pltpu.HBM}
    arrays = [pltpu.with_memory_space_constraint(a, spaces[w]) if w else a for a, w in ins]
    moved = sum(a.size * a.dtype.itemsize for a, _ in ins)
    moved += sum(math.prod(shape) * jnp.dtype(kind).itemsize for shape, kind, _ in outs)

    def spec(where):
        return pl.BlockSpec(memory_space=pl.ANY if where == "hbm" else pltpu.VMEM)

    return pl.pallas_call(
        kernel,
        name=name,
        in_specs=[spec(w) for _, w in ins],
        out_specs=[spec("hbm" if w == "hbm raw" else "") for _, _, w in outs],
        out_shape=[
            spaces["hbm" if w == "hbm raw" else w](shape, kind) if w else jax.ShapeDtypeStruct(shape, kind)
            for shape, kind, w in outs
        ],
        scratch_shapes=scratch,
        input_output_aliases=aliases or {},
        cost_estimate=pl.CostEstimate(flops=flops, bytes_accessed=moved, transcendentals=0),
        compiler_params=pltpu.CompilerParams(vmem_limit_bytes=VMEM_GRANT),
    )(*arrays)


def fetch(pairs, sems):
    copies = [pltpu.make_async_copy(src, dst, sems.at[i]) for i, (src, dst) in enumerate(pairs)]
    for copy in copies:
        copy.start()
    return copies


def attend_within(q_ref, k_ref, v_ref, within_ref):
    for head in range(q_ref.shape[1] // DH):
        at = columns(head)
        upper, lower = halves(causal(dot(q_ref[:, at], k_ref[:, at], 1, 1)))
        v = v_ref[:, at]
        within_ref[:, at] = dot(upper, v) + dot(lower, v)


def states_kernel(q_hbm, k_hbm, v_hbm, dy_hbm, gain_hbm, state_ref, within_ref, q_ref, dy_ref, gain_ref, k_ref, v_ref, sems):
    first = lax.axis_index("dp") == 0
    near = fetch(((k_hbm, k_ref), (v_hbm, v_ref)), sems)
    later = [
        pltpu.make_async_copy(src, dst, sems.at[2 + i])
        for i, (src, dst) in enumerate(((q_hbm, q_ref), (dy_hbm, dy_ref), (gain_hbm, gain_ref)))
    ]

    @pl.when(first)
    def _():
        for copy in later:
            copy.start()

    for copy in near:
        copy.wait()
    for head in range(k_ref.shape[1] // DH):
        at = columns(head)
        state_ref[at, :] = dot(k_ref[:, at], v_ref[:, at], 0, 0)

    @pl.when(first)
    def _():
        for copy in later:
            copy.wait()
        attend_within(q_ref, k_ref, v_ref, within_ref)


def within_kernel(q_hbm, k_hbm, v_hbm, dy_hbm, gain_hbm, *refs):
    within_ref, q_ref, dy_ref, gain_ref, k_ref, v_ref, sems = refs[4:]

    @pl.when(lax.axis_index("dp") != 0)
    def _():
        copies = fetch(
            ((q_hbm, q_ref), (k_hbm, k_ref), (v_hbm, v_ref), (dy_hbm, dy_ref), (gain_hbm, gain_ref)), sems
        )
        for copy in copies:
            copy.wait()
        attend_within(q_ref, k_ref, v_ref, within_ref)


def scan(part_ref, out_ref, out_hbm, sems, reverse):
    count, rows = part_ref.shape[0], out_ref.shape[1]
    group = count // sems.shape[0]
    total = jnp.zeros(out_ref.shape[1:], F32)
    copies = []
    for i in range(count):
        place = count - 1 - i if reverse else i
        out_ref[place] = total
        total = total + part_ref[place, :rows]
        if i % group == group - 1:
            at = pl.ds(place if reverse else place + 1 - group, group)
            copies.append(pltpu.make_async_copy(out_ref.at[at], out_hbm.at[at], sems.at[len(copies)]))
            copies[-1].start()
    return copies


def prefix_kernel(part_ref, out_hbm, out_ref, sems):
    for copy in scan(part_ref, out_ref, out_hbm, sems, False):
        copy.wait()


def suffix_kernel(gain_scale, part_ref, _, out_hbm, gain_ref, out_ref, sems):
    copies = scan(part_ref, out_ref, out_hbm, sems, True)
    rows = out_ref.shape[1]
    gain = jnp.zeros(gain_ref.shape, F32)
    for i in range(part_ref.shape[0]):
        gain = gain + part_ref[i, rows:]
    gain_ref[...] = gain_scale * gain
    for copy in copies:
        copy.wait()


def attend_kernel(scale, q_ref, within_ref, state_ref, gain_ref, dy_ref, attn_ref, sums_ref):
    tokens = q_ref.shape[0]
    squares = jnp.zeros((tokens, DH), F32)
    inner = jnp.zeros((tokens, DH), F32)
    for head in range(q_ref.shape[1] // DH):
        at = columns(head)
        q = q_ref[:, at]
        upper, lower = halves(state_ref[at, :])
        before = dot(jnp.concatenate([q, q], 1), jnp.concatenate([upper, lower], 0))
        attn = scale * (within_ref[:, at] + before)
        attn_ref[:, at] = attn
        squares += attn * attn
        inner += (gain_ref[:, at] * dy_ref[:, at].astype(F32)) * attn
    row = lax.broadcasted_iota(jnp.int32, (8, tokens), 0)
    sums = jnp.where(
        row == 0,
        jnp.sum(squares.T, axis=0, keepdims=True),
        jnp.where(row == 1, jnp.sum(inner.T, axis=0, keepdims=True), 0.0),
    )
    for i in range(sums_ref.shape[0]):
        sums_ref[i] = sums


def token_factors(sums_ref, width):
    sums = sums_ref[0]
    for i in range(1, sums_ref.shape[0]):
        sums = sums + sums_ref[i]
    inverse = 1.0 / jnp.sqrt(sums[0:1] / width + epsilon)
    other = sums[1:2] * (inverse * inverse * inverse) / width
    row = lax.broadcasted_iota(jnp.int32, sums.shape, 0)
    both = jnp.where(row == 0, inverse, other).T
    return tuple(jnp.broadcast_to(both[:, i : i + 1], (both.shape[0], DH)) for i in range(2))


def grad_state_kernel(width, sums_ref, q_ref, attn_ref, gain_ref, dy_ref, state_hbm, factor_ref, state_ref, sems):
    inverse, other = token_factors(sums_ref, width)
    factor_ref[0] = inverse
    factor_ref[1] = other
    heads = q_ref.shape[1] // DH
    per_head = state_ref.shape[0] // heads
    rows = DH // per_head
    copies = []

    def send(slices, part):
        at = (slices, part)
        copies.append(pltpu.make_async_copy(state_ref.at[at], state_hbm.at[at], sems.at[len(copies)]))
        copies[-1].start()

    weights = []
    for head in range(heads):
        at = columns(head)
        weights.append(jnp.sum(dy_ref[:, at].astype(F32) * (attn_ref[:, at] * inverse), axis=0, keepdims=True))
    weights = jnp.concatenate(weights, 0)
    for i in range(state_ref.shape[0]):
        state_ref[i, rows:, :] = weights
    send(pl.ds(0, state_ref.shape[0]), pl.ds(rows, heads))
    for head in range(heads):
        at = columns(head)
        d_attn = (gain_ref[:, at] * dy_ref[:, at].astype(F32)) * inverse - attn_ref[:, at] * other
        upper, lower = halves(d_attn)
        q = q_ref[:, at]
        state = dot(q, upper, 0, 0) + dot(q, lower, 0, 0)
        state_ref[head * per_head : (head + 1) * per_head, :rows, :] = state.reshape(per_head, rows, DH)
        if head % 2:
            send(pl.ds((head - 1) * per_head, 2 * per_head), pl.ds(0, rows))
    for copy in copies:
        copy.wait()


def backward_kernel(scale, q_hbm, k_hbm, v_hbm, dy_hbm, gain_ref, attn_ref, state_ref, factor_ref, out_ref, dq_ref, dk_ref, dv_ref, k_ref, v_ref, q_ref, dy_ref, sems):
    copies = fetch(((q_hbm, q_ref), (k_hbm, k_ref), (v_hbm, v_ref), (dy_hbm, dy_ref)), sems)
    for copy in copies:
        copy.wait()
    inverse = factor_ref[0]
    other = factor_ref[1]
    for head in range(q_ref.shape[1] // DH):
        at = columns(head)
        q, k, v = q_ref[:, at], k_ref[:, at], v_ref[:, at]
        gain = gain_ref[:, at]
        attn = attn_ref[:, at]
        out_ref[:, at] = (gain * (attn * inverse)).astype(out_ref.dtype)
        d_attn = (gain * dy_ref[:, at].astype(F32)) * inverse - attn * other
        d_upper, d_lower = halves(d_attn)
        d_both = jnp.concatenate([d_upper, d_lower], 1)
        s_upper, s_lower = halves(causal(dot(q, k, 1, 1)))
        ds_upper, ds_lower = halves(causal(dot(d_both, jnp.concatenate([v, v], 1), 1, 1)))
        p_upper, p_lower = halves(state_ref[at, :])
        dq = dot(ds_upper, k) + dot(ds_lower, k)
        dq += dot(d_both, jnp.concatenate([p_upper, p_upper], 1), 1, 1)
        dq += dot(d_upper, p_lower, 1, 1)
        dq_ref[:, at] = (scale * dq).astype(dq_ref.dtype)
        dk_ref[:, at] = dot(ds_upper, q, 0, 0) + dot(ds_lower, q, 0, 0)
        dv_ref[:, at] = dot(s_upper, d_upper, 0, 0) + dot(s_upper, d_lower, 0, 0) + dot(s_lower, d_upper, 0, 0)


def return_kernel(k_hbm, v_hbm, dk_hbm, dv_hbm, gain_a, gain_b, _, k_ref, v_ref, dk_ref, dv_ref, gain_ref, sems):
    v_half = v_hbm.at[:, pl.ds(0, v_ref.shape[1])]
    copies = fetch(((k_hbm, k_ref), (v_half, v_ref), (dk_hbm, dk_ref), (dv_hbm, dv_ref)), sems)
    gain_ref[...] = gain_a[...] + gain_b[...]
    for copy in copies:
        copy.wait()


def last_kernel(scale, k_ref, v_near, v_hbm, state_ref, dk_in, dv_in, dk_hbm, dv_hbm, v_far, dk_ref, dv_ref, sems):
    wide = v_near.shape[1]
    heads = k_ref.shape[1] // DH
    half = heads // 2
    v_copy = pltpu.make_async_copy(v_hbm.at[:, pl.ds(wide, wide)], v_far, sems.at[4])
    v_copy.start()
    copies = []

    def store(src, dst, part):
        at = pl.ds(part * wide, wide)
        copies.append(pltpu.make_async_copy(src.at[:, at], dst.at[:, at], sems.at[len(copies)]))
        copies[-1].start()

    states = []
    for head in range(heads):
        at = columns(head)
        upper, lower = halves(state_ref[at, :])
        states.append((upper, lower))
        k = k_ref[:, at]
        dv = dv_in[:, at] + dot(jnp.concatenate([k, k], 1), jnp.concatenate([upper, lower], 0))
        dv_ref[:, at] = (scale * dv).astype(dv_ref.dtype)
        if head % half == half - 1:
            store(dv_ref, dv_hbm, head // half)
    for head in range(heads):
        at = columns(head)
        if head == half:
            v_copy.wait()
        v = v_near[:, at] if head < half else v_far[:, columns(head - half)]
        dk = dk_in[:, at] + dot(jnp.concatenate([v, v], 1), jnp.concatenate(states[head], 1), 1, 1)
        dk_ref[:, at] = (scale * dk).astype(dk_ref.dtype)
        if head % half == half - 1:
            store(dk_ref, dk_hbm, head // half)
    for copy in copies:
        copy.wait()


def body(queries, keys, values, gain, grad_out):
    _, tokens, wide = queries.shape
    q, k, v, dy = (a.reshape(tokens, wide) for a in (queries, keys, values, grad_out))
    gain = gain.reshape(1, wide)
    heads = wide // DH
    ctx, shards = lax.axis_size("ctx"), lax.axis_size("heads")
    width = float(shards * wide)
    scale = DH ** (-0.5)
    rows = wide // ctx
    per = 2 * tokens * DH * DH * heads
    all_tok = (tokens, wide)
    exchange = functools.partial(lax.all_to_all, axis_name="ctx", split_axis=0, concat_axis=0, tiled=True)

    inputs = [(a, "hbm") for a in (q, k, v, dy, gain)]
    near = [(all_tok, F32, "vmem"), (all_tok, BF16, "vmem"), (all_tok, BF16, "vmem"), ((1, wide), F32, "vmem")]
    inner = [pltpu.VMEM(all_tok, BF16), pltpu.VMEM(all_tok, BF16), pltpu.SemaphoreType.DMA((5,))]
    local, *held = call(states_kernel, "key_value_states", inputs, [((wide, DH), F32, "")] + near, 4 * per, inner)
    parts = exchange(local).reshape(ctx, rows, DH)
    within, q_near, dy_near, gain_near = call(
        within_kernel,
        "within_block",
        inputs + [(a, "vmem") for a in held],
        near,
        6 * per,
        inner,
        {len(inputs) + i: i for i in range(len(held))},
    )
    scan_room = [pltpu.VMEM((ctx, rows, DH), F32), pltpu.SemaphoreType.DMA((4,))]
    (before,) = call(
        prefix_kernel, "prefix", [(parts, "")], [((ctx, rows, DH), F32, "hbm raw")], wide * DH, scan_room
    )
    prefix = exchange(before.reshape(wide, DH))
    attn, sums = call(
        functools.partial(attend_kernel, scale),
        "attend",
        [(q_near, "vmem"), (within, "vmem"), (prefix, ""), (gain_near, "vmem"), (dy_near, "vmem")],
        [(all_tok, F32, "vmem"), ((shards, 8, tokens), F32, "")],
        2 * per,
    )
    sums = lax.all_to_all(sums, "heads", 0, 0, tiled=True)
    grad_local, factors = call(
        functools.partial(grad_state_kernel, width),
        "grad_states",
        [(sums, ""), (q_near, "vmem"), (attn, "vmem"), (gain_near, "vmem"), (dy_near, "vmem")],
        [((ctx, rows + heads, DH), F32, "hbm raw"), ((2, tokens, DH), F32, "vmem")],
        2 * per,
        [pltpu.VMEM((ctx, rows + heads, DH), F32), pltpu.SemaphoreType.DMA((heads // 2 + 1,))],
    )
    grad_parts = exchange(grad_local)
    output, d_query, dk_part, dv_part = call(
        functools.partial(backward_kernel, scale),
        "backward_within",
        [(q, "hbm"), (k, "hbm"), (v, "hbm"), (dy, "hbm"), (gain_near, "vmem"), (attn, "vmem"), (prefix, ""), (factors, "vmem")],
        [(all_tok, BF16, "hbm"), (all_tok, BF16, "hbm"), (all_tok, F32, "hbm"), (all_tok, F32, "hbm")],
        22 * per,
        [pltpu.VMEM(all_tok, BF16)] * 4 + [pltpu.SemaphoreType.DMA((4,))],
    )
    total_rows = lax.axis_size("dp") * ctx * tokens
    after, gain_sum = call(
        functools.partial(suffix_kernel, 1.0 / math.sqrt(total_rows)),
        "suffix",
        [(grad_parts, ""), (dv_part, "hbm")],
        [((ctx, rows, DH), F32, "hbm raw"), ((heads, DH), F32, "")],
        wide * DH,
        scan_room,
    )
    suffix = exchange(after.reshape(wide, DH))
    gain_other = lax.ppermute(gain_sum, "dp", [(i, lax.axis_size("dp") - 1 - i) for i in range(lax.axis_size("dp"))])
    k_near, v_near, dk_near, dv_near, grad_gain = call(
        return_kernel,
        "return_operands",
        [(k, "hbm"), (v, "hbm"), (dk_part, "hbm"), (dv_part, "hbm"), (gain_sum, ""), (gain_other, ""), (after, "hbm")],
        [(all_tok, BF16, "vmem"), ((tokens, wide // 2), BF16, "vmem"), (all_tok, F32, "vmem"), (all_tok, F32, "vmem"), ((heads, DH), F32, "hbm")],
        wide * DH,
        [pltpu.SemaphoreType.DMA((4,))],
    )
    d_key, d_value = call(
        functools.partial(last_kernel, scale),
        "key_value_gradients",
        [(k_near, "vmem"), (v_near, "vmem"), (v, "hbm"), (suffix, ""), (dk_near, "vmem"), (dv_near, "vmem")],
        [(all_tok, BF16, "hbm raw"), (all_tok, BF16, "hbm raw")],
        4 * per,
        [pltpu.VMEM((tokens, wide // 2), BF16)] + [pltpu.VMEM(all_tok, BF16)] * 2 + [pltpu.SemaphoreType.DMA((5,))],
    )
    return (*(a[None] for a in (output, d_query, d_key, d_value)), grad_gain.reshape(wide))


def solution(mesh):
    placed = P("dp", "ctx", "heads")
    return jax.shard_map(
        body,
        mesh=mesh,
        in_specs=(placed, placed, placed, P("heads"), placed),
        out_specs=(placed, placed, placed, placed, P("heads")),
        check_vma=False,
    )
```

```python
import functools
import math

import jax
import jax.numpy as jnp
from jax import lax
from jax.experimental import pallas as pl
from jax.experimental.pallas import tpu as pltpu
from jax.sharding import PartitionSpec as P

DH = 128
epsilon = 1e-05
F32 = jnp.float32
BF16 = jnp.bfloat16
VMEM_GRANT = 16 * 1024 * 1024
SUFFIX_OUT = "hbm"


def halves(x):
    upper = x.astype(BF16)
    return upper, (x - upper.astype(F32)).astype(BF16)


def dot(a, b, ca=1, cb=0):
    return lax.dot_general(a, b, (((ca,), (cb,)), ((), ())), preferred_element_type=F32)


def columns(head):
    return slice(head * DH, (head + 1) * DH)


def causal(x):
    row = lax.broadcasted_iota(jnp.int32, x.shape, 0)
    column = lax.broadcasted_iota(jnp.int32, x.shape, 1)
    return jnp.where(row >= column, x, 0.0)


def call(kernel, name, ins, outs, flops, scratch=(), aliases=None):
    spaces = {"vmem": pltpu.VMEM, "hbm": pltpu.HBM}
    arrays = [pltpu.with_memory_space_constraint(a, spaces[w]) if w else a for a, w in ins]
    moved = sum(a.size * a.dtype.itemsize for a, _ in ins)
    moved += sum(math.prod(shape) * jnp.dtype(kind).itemsize for shape, kind, _ in outs)

    def spec(where):
        return pl.BlockSpec(memory_space=pl.ANY if where == "hbm" else pltpu.VMEM)

    return pl.pallas_call(
        kernel,
        name=name,
        in_specs=[spec(w) for _, w in ins],
        out_specs=[spec("hbm" if w == "hbm raw" else "") for _, _, w in outs],
        out_shape=[
            spaces["hbm" if w == "hbm raw" else w](shape, kind) if w else jax.ShapeDtypeStruct(shape, kind)
            for shape, kind, w in outs
        ],
        scratch_shapes=scratch,
        input_output_aliases=aliases or {},
        cost_estimate=pl.CostEstimate(flops=flops, bytes_accessed=moved, transcendentals=0),
        compiler_params=pltpu.CompilerParams(vmem_limit_bytes=VMEM_GRANT),
    )(*arrays)


def fetch(pairs, sems):
    copies = [pltpu.make_async_copy(src, dst, sems.at[i]) for i, (src, dst) in enumerate(pairs)]
    for copy in copies:
        copy.start()
    return copies


def attend_within(q_ref, k_ref, v_ref, within_ref):
    for head in range(q_ref.shape[1] // DH):
        at = columns(head)
        upper, lower = halves(causal(dot(q_ref[:, at], k_ref[:, at], 1, 1)))
        v = v_ref[:, at]
        within_ref[:, at] = dot(upper, v) + dot(lower, v)


def states_kernel(q_hbm, k_hbm, v_hbm, dy_hbm, gain_hbm, state_ref, within_ref, q_ref, dy_ref, gain_ref, k_ref, v_ref, sems):
    for copy in fetch(((k_hbm, k_ref), (v_hbm, v_ref)), sems):
        copy.wait()
    for head in range(k_ref.shape[1] // DH):
        at = columns(head)
        state_ref[at, :] = dot(k_ref[:, at], v_ref[:, at], 0, 0)

    @pl.when(lax.axis_index("dp") == 0)
    def _():
        for copy in fetch(((q_hbm, q_ref), (dy_hbm, dy_ref), (gain_hbm, gain_ref)), sems):
            copy.wait()
        attend_within(q_ref, k_ref, v_ref, within_ref)


def within_kernel(q_hbm, k_hbm, v_hbm, dy_hbm, gain_hbm, *refs):
    within_ref, q_ref, dy_ref, gain_ref, k_ref, v_ref, sems = refs[4:]

    @pl.when(lax.axis_index("dp") != 0)
    def _():
        copies = fetch(
            ((q_hbm, q_ref), (k_hbm, k_ref), (v_hbm, v_ref), (dy_hbm, dy_ref), (gain_hbm, gain_ref)), sems
        )
        for copy in copies:
            copy.wait()
        attend_within(q_ref, k_ref, v_ref, within_ref)


def scan(part_ref, out_ref, out_hbm, sems, reverse):
    count, rows = part_ref.shape[0], out_ref.shape[1]
    group = count // sems.shape[0]
    total = jnp.zeros(out_ref.shape[1:], F32)
    copies = []
    for i in range(count):
        place = count - 1 - i if reverse else i
        out_ref[place] = total
        total = total + part_ref[place, :rows]
        if i % group == group - 1:
            at = pl.ds(place if reverse else place + 1 - group, group)
            copies.append(pltpu.make_async_copy(out_ref.at[at], out_hbm.at[at], sems.at[len(copies)]))
            copies[-1].start()
    return copies


def prefix_kernel(part_ref, out_hbm, out_ref, sems):
    for copy in scan(part_ref, out_ref, out_hbm, sems, False):
        copy.wait()


def suffix_kernel(gain_scale, part_ref, _, out_hbm, gain_ref, out_ref, sems):
    copies = scan(part_ref, out_ref, out_hbm, sems, True)
    rows = out_ref.shape[1]
    gain = jnp.zeros(gain_ref.shape, F32)
    for i in range(part_ref.shape[0]):
        gain = gain + part_ref[i, rows:]
    gain_ref[...] = gain_scale * gain
    for copy in copies:
        copy.wait()


def attend_kernel(scale, q_ref, within_ref, state_ref, gain_ref, dy_ref, attn_ref, sums_ref):
    tokens = q_ref.shape[0]
    squares = jnp.zeros((tokens, DH), F32)
    inner = jnp.zeros((tokens, DH), F32)
    for head in range(q_ref.shape[1] // DH):
        at = columns(head)
        q = q_ref[:, at]
        upper, lower = halves(state_ref[at, :])
        before = dot(jnp.concatenate([q, q], 1), jnp.concatenate([upper, lower], 0))
        attn = scale * (within_ref[:, at] + before)
        attn_ref[:, at] = attn
        squares += attn * attn
        inner += (gain_ref[:, at] * dy_ref[:, at].astype(F32)) * attn
    row = lax.broadcasted_iota(jnp.int32, (8, tokens), 0)
    sums = jnp.where(
        row == 0,
        jnp.sum(squares.T, axis=0, keepdims=True),
        jnp.where(row == 1, jnp.sum(inner.T, axis=0, keepdims=True), 0.0),
    )
    for i in range(sums_ref.shape[0]):
        sums_ref[i] = sums


def token_factors(sums_ref, width):
    sums = sums_ref[0]
    for i in range(1, sums_ref.shape[0]):
        sums = sums + sums_ref[i]
    inverse = 1.0 / jnp.sqrt(sums[0:1] / width + epsilon)
    other = sums[1:2] * (inverse * inverse * inverse) / width
    row = lax.broadcasted_iota(jnp.int32, sums.shape, 0)
    both = jnp.where(row == 0, inverse, other).T
    return tuple(jnp.broadcast_to(both[:, i : i + 1], (both.shape[0], DH)) for i in range(2))


def grad_state_kernel(width, sums_ref, q_ref, attn_ref, gain_ref, dy_ref, state_hbm, factor_ref, state_ref, sems):
    inverse, other = token_factors(sums_ref, width)
    factor_ref[0] = inverse
    factor_ref[1] = other
    heads = q_ref.shape[1] // DH
    per_head = state_ref.shape[0] // heads
    rows = DH // per_head
    copies = []

    def send(slices, part):
        at = (slices, part)
        copies.append(pltpu.make_async_copy(state_ref.at[at], state_hbm.at[at], sems.at[len(copies)]))
        copies[-1].start()

    weights = []
    for head in range(heads):
        at = columns(head)
        weights.append(jnp.sum(dy_ref[:, at].astype(F32) * (attn_ref[:, at] * inverse), axis=0, keepdims=True))
    weights = jnp.concatenate(weights, 0)
    for i in range(state_ref.shape[0]):
        state_ref[i, rows:, :] = weights
    send(pl.ds(0, state_ref.shape[0]), pl.ds(rows, heads))
    for head in range(heads):
        at = columns(head)
        d_attn = (gain_ref[:, at] * dy_ref[:, at].astype(F32)) * inverse - attn_ref[:, at] * other
        upper, lower = halves(d_attn)
        q = q_ref[:, at]
        state = dot(q, upper, 0, 0) + dot(q, lower, 0, 0)
        state_ref[head * per_head : (head + 1) * per_head, :rows, :] = state.reshape(per_head, rows, DH)
        if head % 2:
            send(pl.ds((head - 1) * per_head, 2 * per_head), pl.ds(0, rows))
    for copy in copies:
        copy.wait()


def backward_kernel(scale, q_hbm, k_hbm, v_hbm, dy_hbm, gain_ref, attn_ref, state_ref, factor_ref, out_ref, dq_ref, dk_ref, dv_ref, k_ref, v_ref, q_ref, dy_ref, sems):
    copies = fetch(((q_hbm, q_ref), (k_hbm, k_ref), (v_hbm, v_ref), (dy_hbm, dy_ref)), sems)
    for copy in copies:
        copy.wait()
    inverse = factor_ref[0]
    other = factor_ref[1]
    for head in range(q_ref.shape[1] // DH):
        at = columns(head)
        q, k, v = q_ref[:, at], k_ref[:, at], v_ref[:, at]
        gain = gain_ref[:, at]
        attn = attn_ref[:, at]
        out_ref[:, at] = (gain * (attn * inverse)).astype(out_ref.dtype)
        d_attn = (gain * dy_ref[:, at].astype(F32)) * inverse - attn * other
        d_upper, d_lower = halves(d_attn)
        d_both = jnp.concatenate([d_upper, d_lower], 1)
        s_upper, s_lower = halves(causal(dot(q, k, 1, 1)))
        ds_upper, ds_lower = halves(causal(dot(d_both, jnp.concatenate([v, v], 1), 1, 1)))
        p_upper, p_lower = halves(state_ref[at, :])
        dq = dot(ds_upper, k) + dot(ds_lower, k)
        dq += dot(d_both, jnp.concatenate([p_upper, p_upper], 1), 1, 1)
        dq += dot(d_upper, p_lower, 1, 1)
        dq_ref[:, at] = (scale * dq).astype(dq_ref.dtype)
        dk_ref[:, at] = dot(ds_upper, q, 0, 0) + dot(ds_lower, q, 0, 0)
        dv_ref[:, at] = dot(s_upper, d_upper, 0, 0) + dot(s_upper, d_lower, 0, 0) + dot(s_lower, d_upper, 0, 0)


def return_kernel(k_hbm, v_hbm, dk_hbm, dv_hbm, gain_a, gain_b, _, k_ref, v_ref, dk_ref, dv_ref, gain_ref, sems):
    v_half = v_hbm.at[:, pl.ds(0, v_ref.shape[1])]
    copies = fetch(((k_hbm, k_ref), (v_half, v_ref), (dk_hbm, dk_ref), (dv_hbm, dv_ref)), sems)
    gain_ref[...] = gain_a[...] + gain_b[...]
    for copy in copies:
        copy.wait()


def last_kernel(scale, k_ref, v_near, v_hbm, state_ref, dk_in, dv_in, dk_hbm, dv_hbm, v_far, dk_ref, dv_ref, sems):
    wide = v_near.shape[1]
    heads = k_ref.shape[1] // DH
    half = heads // 2
    v_copy = pltpu.make_async_copy(v_hbm.at[:, pl.ds(wide, wide)], v_far, sems.at[4])
    v_copy.start()
    copies = []

    def store(src, dst, part):
        at = pl.ds(part * wide, wide)
        copies.append(pltpu.make_async_copy(src.at[:, at], dst.at[:, at], sems.at[len(copies)]))
        copies[-1].start()

    states = []
    for head in range(heads):
        at = columns(head)
        upper, lower = halves(state_ref[at, :])
        states.append((upper, lower))
        k = k_ref[:, at]
        dv = dv_in[:, at] + dot(jnp.concatenate([k, k], 1), jnp.concatenate([upper, lower], 0))
        dv_ref[:, at] = (scale * dv).astype(dv_ref.dtype)
        if head % half == half - 1:
            store(dv_ref, dv_hbm, head // half)
    for head in range(heads):
        at = columns(head)
        if head == half:
            v_copy.wait()
        v = v_near[:, at] if head < half else v_far[:, columns(head - half)]
        dk = dk_in[:, at] + dot(jnp.concatenate([v, v], 1), jnp.concatenate(states[head], 1), 1, 1)
        dk_ref[:, at] = (scale * dk).astype(dk_ref.dtype)
        if head % half == half - 1:
            store(dk_ref, dk_hbm, head // half)
    for copy in copies:
        copy.wait()


def body(queries, keys, values, gain, grad_out):
    _, tokens, wide = queries.shape
    q, k, v, dy = (a.reshape(tokens, wide) for a in (queries, keys, values, grad_out))
    gain = gain.reshape(1, wide)
    heads = wide // DH
    ctx, shards = lax.axis_size("ctx"), lax.axis_size("heads")
    width = float(shards * wide)
    scale = DH ** (-0.5)
    rows = wide // ctx
    per = 2 * tokens * DH * DH * heads
    all_tok = (tokens, wide)
    exchange = functools.partial(lax.all_to_all, axis_name="ctx", split_axis=0, concat_axis=0, tiled=True)

    inputs = [(a, "hbm") for a in (q, k, v, dy, gain)]
    near = [(all_tok, F32, "vmem"), (all_tok, BF16, "vmem"), (all_tok, BF16, "vmem"), ((1, wide), F32, "vmem")]
    inner = [pltpu.VMEM(all_tok, BF16), pltpu.VMEM(all_tok, BF16), pltpu.SemaphoreType.DMA((5,))]
    local, *held = call(states_kernel, "key_value_states", inputs, [((wide, DH), F32, "")] + near, 4 * per, inner)
    parts = exchange(local).reshape(ctx, rows, DH)
    within, q_near, dy_near, gain_near = call(
        within_kernel,
        "within_block",
        inputs + [(a, "vmem") for a in held],
        near,
        6 * per,
        inner,
        {len(inputs) + i: i for i in range(len(held))},
    )
    scan_room = [pltpu.VMEM((ctx, rows, DH), F32), pltpu.SemaphoreType.DMA((4,))]
    (before,) = call(
        prefix_kernel, "prefix", [(parts, "")], [((ctx, rows, DH), F32, "hbm raw")], wide * DH, scan_room
    )
    prefix = exchange(before.reshape(wide, DH))
    attn, sums = call(
        functools.partial(attend_kernel, scale),
        "attend",
        [(q_near, "vmem"), (within, "vmem"), (prefix, ""), (gain_near, "vmem"), (dy_near, "vmem")],
        [(all_tok, F32, "vmem"), ((shards, 8, tokens), F32, "")],
        2 * per,
    )
    sums = lax.all_to_all(sums, "heads", 0, 0, tiled=True)
    grad_local, factors = call(
        functools.partial(grad_state_kernel, width),
        "grad_states",
        [(sums, ""), (q_near, "vmem"), (attn, "vmem"), (gain_near, "vmem"), (dy_near, "vmem")],
        [((ctx, rows + heads, DH), F32, "hbm raw"), ((2, tokens, DH), F32, "vmem")],
        2 * per,
        [pltpu.VMEM((ctx, rows + heads, DH), F32), pltpu.SemaphoreType.DMA((heads // 2 + 1,))],
    )
    grad_parts = exchange(grad_local)
    output, d_query, dk_part, dv_part = call(
        functools.partial(backward_kernel, scale),
        "backward_within",
        [(q, "hbm"), (k, "hbm"), (v, "hbm"), (dy, "hbm"), (gain_near, "vmem"), (attn, "vmem"), (prefix, ""), (factors, "vmem")],
        [(all_tok, BF16, "hbm"), (all_tok, BF16, "hbm"), (all_tok, F32, "hbm"), (all_tok, F32, "hbm")],
        22 * per,
        [pltpu.VMEM(all_tok, BF16)] * 4 + [pltpu.SemaphoreType.DMA((4,))],
    )
    total_rows = lax.axis_size("dp") * ctx * tokens
    after, gain_sum = call(
        functools.partial(suffix_kernel, 1.0 / math.sqrt(total_rows)),
        "suffix",
        [(grad_parts, ""), (dv_part, "hbm")],
        [((ctx, rows, DH), F32, "hbm raw"), ((heads, DH), F32, "")],
        wide * DH,
        scan_room,
    )
    suffix = exchange(after.reshape(wide, DH))
    gain_other = lax.ppermute(gain_sum, "dp", [(i, lax.axis_size("dp") - 1 - i) for i in range(lax.axis_size("dp"))])
    k_near, v_near, dk_near, dv_near, grad_gain = call(
        return_kernel,
        "return_operands",
        [(k, "hbm"), (v, "hbm"), (dk_part, "hbm"), (dv_part, "hbm"), (gain_sum, ""), (gain_other, ""), (after, "hbm")],
        [(all_tok, BF16, "vmem"), ((tokens, wide // 2), BF16, "vmem"), (all_tok, F32, "vmem"), (all_tok, F32, "vmem"), ((heads, DH), F32, "hbm")],
        wide * DH,
        [pltpu.SemaphoreType.DMA((4,))],
    )
    d_key, d_value = call(
        functools.partial(last_kernel, scale),
        "key_value_gradients",
        [(k_near, "vmem"), (v_near, "vmem"), (v, "hbm"), (suffix, ""), (dk_near, "vmem"), (dv_near, "vmem")],
        [(all_tok, BF16, "hbm raw"), (all_tok, BF16, "hbm raw")],
        4 * per,
        [pltpu.VMEM((tokens, wide // 2), BF16)] + [pltpu.VMEM(all_tok, BF16)] * 2 + [pltpu.SemaphoreType.DMA((5,))],
    )
    return (*(a[None] for a in (output, d_query, d_key, d_value)), grad_gain.reshape(wide))


def solution(mesh):
    placed = P("dp", "ctx", "heads")
    return jax.shard_map(
        body,
        mesh=mesh,
        in_specs=(placed, placed, placed, P("heads"), placed),
        out_specs=(placed, placed, placed, placed, P("heads")),
        check_vma=False,
    )
```

```python
import functools
import math

import jax
import jax.numpy as jnp
from jax import lax
from jax.experimental import pallas as pl
from jax.experimental.pallas import tpu as pltpu
from jax.sharding import PartitionSpec as P

DH = 128
epsilon = 1e-05
F32 = jnp.float32
BF16 = jnp.bfloat16
VMEM_GRANT = 16 * 1024 * 1024
SUFFIX_OUT = "hbm"


def halves(x):
    upper = x.astype(BF16)
    return upper, (x - upper.astype(F32)).astype(BF16)


def dot(a, b, ca=1, cb=0):
    return lax.dot_general(a, b, (((ca,), (cb,)), ((), ())), preferred_element_type=F32)


def columns(head):
    return slice(head * DH, (head + 1) * DH)


def causal(x):
    row = lax.broadcasted_iota(jnp.int32, x.shape, 0)
    column = lax.broadcasted_iota(jnp.int32, x.shape, 1)
    return jnp.where(row >= column, x, 0.0)


def call(kernel, name, ins, outs, flops, scratch=(), aliases=None):
    spaces = {"vmem": pltpu.VMEM, "hbm": pltpu.HBM}
    arrays = [pltpu.with_memory_space_constraint(a, spaces[w]) if w else a for a, w in ins]
    moved = sum(a.size * a.dtype.itemsize for a, _ in ins)
    moved += sum(math.prod(shape) * jnp.dtype(kind).itemsize for shape, kind, _ in outs)

    def spec(where):
        return pl.BlockSpec(memory_space=pl.ANY if where == "hbm" else pltpu.VMEM)

    return pl.pallas_call(
        kernel,
        name=name,
        in_specs=[spec(w) for _, w in ins],
        out_specs=[spec("hbm" if w == "hbm raw" else "") for _, _, w in outs],
        out_shape=[
            spaces["hbm" if w == "hbm raw" else w](shape, kind) if w else jax.ShapeDtypeStruct(shape, kind)
            for shape, kind, w in outs
        ],
        scratch_shapes=scratch,
        input_output_aliases=aliases or {},
        cost_estimate=pl.CostEstimate(flops=flops, bytes_accessed=moved, transcendentals=0),
        compiler_params=pltpu.CompilerParams(vmem_limit_bytes=VMEM_GRANT),
    )(*arrays)


def fetch(pairs, sems):
    copies = [pltpu.make_async_copy(src, dst, sems.at[i]) for i, (src, dst) in enumerate(pairs)]
    for copy in copies:
        copy.start()
    return copies


def attend_within(q_ref, k_ref, v_ref, within_ref):
    for head in range(q_ref.shape[1] // DH):
        at = columns(head)
        upper, lower = halves(causal(dot(q_ref[:, at], k_ref[:, at], 1, 1)))
        v = v_ref[:, at]
        within_ref[:, at] = dot(upper, v) + dot(lower, v)


def states_kernel(q_hbm, k_hbm, v_hbm, dy_hbm, gain_hbm, state_ref, within_ref, q_ref, dy_ref, gain_ref, k_ref, v_ref, sems):
    for copy in fetch(((k_hbm, k_ref), (v_hbm, v_ref)), sems):
        copy.wait()
    for head in range(k_ref.shape[1] // DH):
        at = columns(head)
        state_ref[at, :] = dot(k_ref[:, at], v_ref[:, at], 0, 0)

    @pl.when(lax.axis_index("dp") == 0)
    def _():
        for copy in fetch(((q_hbm, q_ref), (dy_hbm, dy_ref), (gain_hbm, gain_ref)), sems):
            copy.wait()
        attend_within(q_ref, k_ref, v_ref, within_ref)


def within_kernel(q_hbm, k_hbm, v_hbm, dy_hbm, gain_hbm, *refs):
    within_ref, q_ref, dy_ref, gain_ref, k_ref, v_ref, sems = refs[4:]

    @pl.when(lax.axis_index("dp") != 0)
    def _():
        copies = fetch(
            ((q_hbm, q_ref), (k_hbm, k_ref), (v_hbm, v_ref), (dy_hbm, dy_ref), (gain_hbm, gain_ref)), sems
        )
        for copy in copies:
            copy.wait()
        attend_within(q_ref, k_ref, v_ref, within_ref)


def scan(part_ref, out_ref, out_hbm, sems, reverse):
    count, rows = part_ref.shape[0], out_ref.shape[1]
    group = count // sems.shape[0]
    total = jnp.zeros(out_ref.shape[1:], F32)
    copies = []
    for i in range(count):
        place = count - 1 - i if reverse else i
        out_ref[place] = total
        total = total + part_ref[place, :rows]
        if i % group == group - 1:
            at = pl.ds(place if reverse else place + 1 - group, group)
            copies.append(pltpu.make_async_copy(out_ref.at[at], out_hbm.at[at], sems.at[len(copies)]))
            copies[-1].start()
    return copies


def prefix_kernel(part_ref, out_hbm, out_ref, sems):
    for copy in scan(part_ref, out_ref, out_hbm, sems, False):
        copy.wait()


def suffix_kernel(gain_scale, part_ref, _, out_hbm, gain_ref, out_ref, sems):
    copies = scan(part_ref, out_ref, out_hbm, sems, True)
    rows = out_ref.shape[1]
    gain = jnp.zeros(gain_ref.shape, F32)
    for i in range(part_ref.shape[0]):
        gain = gain + part_ref[i, rows:]
    gain_ref[...] = gain_scale * gain
    for copy in copies:
        copy.wait()


def attend_kernel(scale, q_ref, within_ref, state_ref, gain_ref, dy_ref, attn_ref, sums_ref):
    tokens = q_ref.shape[0]
    squares = jnp.zeros((tokens, DH), F32)
    inner = jnp.zeros((tokens, DH), F32)
    for head in range(q_ref.shape[1] // DH):
        at = columns(head)
        q = q_ref[:, at]
        upper, lower = halves(state_ref[at, :])
        before = dot(jnp.concatenate([q, q], 1), jnp.concatenate([upper, lower], 0))
        attn = scale * (within_ref[:, at] + before)
        attn_ref[:, at] = attn
        squares += attn * attn
        inner += (gain_ref[:, at] * dy_ref[:, at].astype(F32)) * attn
    rows = []
    for total in (squares, inner):
        line = jnp.sum(total.T, axis=0, keepdims=True)
        rows += [line[:, i : i + DH] for i in range(0, tokens, DH)]
    sums = jnp.concatenate(rows, 0)
    for i in range(sums_ref.shape[0]):
        sums_ref[i] = sums


def token_factors(sums_ref, width):
    sums = sums_ref[0]
    for i in range(1, sums_ref.shape[0]):
        sums = sums + sums_ref[i]
    count = sums.shape[0] // 2
    inverse = 1.0 / jnp.sqrt(sums[:count] / width + epsilon)
    other = sums[count:] * (inverse * inverse * inverse) / width
    both = jnp.concatenate([inverse, other, jnp.zeros((8 - 2 * count, DH), F32)], 0).T

    def spread(first):
        return jnp.concatenate([jnp.broadcast_to(both[:, i : i + 1], (DH, DH)) for i in range(first, first + count)], 0)

    return spread(0), spread(count)


def grad_state_kernel(width, sums_ref, q_ref, attn_ref, gain_ref, dy_ref, state_hbm, factor_ref, state_ref, sems):
    inverse, other = token_factors(sums_ref, width)
    factor_ref[0] = inverse
    factor_ref[1] = other
    heads = q_ref.shape[1] // DH
    per_head = state_ref.shape[0] // heads
    rows = DH // per_head
    copies = []

    def send(slices, part):
        at = (slices, part)
        copies.append(pltpu.make_async_copy(state_ref.at[at], state_hbm.at[at], sems.at[len(copies)]))
        copies[-1].start()

    weights = []
    for head in range(heads):
        at = columns(head)
        weights.append(jnp.sum(dy_ref[:, at].astype(F32) * (attn_ref[:, at] * inverse), axis=0, keepdims=True))
    weights = jnp.concatenate(weights, 0)
    for i in range(state_ref.shape[0]):
        state_ref[i, rows:, :] = weights
    send(pl.ds(0, state_ref.shape[0]), pl.ds(rows, heads))
    for head in range(heads):
        at = columns(head)
        d_attn = (gain_ref[:, at] * dy_ref[:, at].astype(F32)) * inverse - attn_ref[:, at] * other
        upper, lower = halves(d_attn)
        q = q_ref[:, at]
        state = dot(q, upper, 0, 0) + dot(q, lower, 0, 0)
        state_ref[head * per_head : (head + 1) * per_head, :rows, :] = state.reshape(per_head, rows, DH)
        if head % 2:
            send(pl.ds((head - 1) * per_head, 2 * per_head), pl.ds(0, rows))
    for copy in copies:
        copy.wait()


def backward_kernel(scale, q_hbm, k_hbm, v_hbm, dy_hbm, gain_ref, attn_ref, state_ref, factor_ref, out_ref, dq_ref, dk_ref, dv_ref, k_ref, v_ref, q_ref, dy_ref, sems):
    copies = fetch(((q_hbm, q_ref), (k_hbm, k_ref), (v_hbm, v_ref), (dy_hbm, dy_ref)), sems)
    for copy in copies:
        copy.wait()
    inverse = factor_ref[0]
    other = factor_ref[1]
    for head in range(q_ref.shape[1] // DH):
        at = columns(head)
        q, k, v = q_ref[:, at], k_ref[:, at], v_ref[:, at]
        gain = gain_ref[:, at]
        attn = attn_ref[:, at]
        out_ref[:, at] = (gain * (attn * inverse)).astype(out_ref.dtype)
        d_attn = (gain * dy_ref[:, at].astype(F32)) * inverse - attn * other
        d_upper, d_lower = halves(d_attn)
        d_both = jnp.concatenate([d_upper, d_lower], 1)
        s_upper, s_lower = halves(causal(dot(q, k, 1, 1)))
        ds_upper, ds_lower = halves(causal(dot(d_both, jnp.concatenate([v, v], 1), 1, 1)))
        p_upper, p_lower = halves(state_ref[at, :])
        dq = dot(ds_upper, k) + dot(ds_lower, k)
        dq += dot(d_both, jnp.concatenate([p_upper, p_upper], 1), 1, 1)
        dq += dot(d_upper, p_lower, 1, 1)
        dq_ref[:, at] = (scale * dq).astype(dq_ref.dtype)
        dk_ref[:, at] = dot(ds_upper, q, 0, 0) + dot(ds_lower, q, 0, 0)
        dv_ref[:, at] = dot(s_upper, d_upper, 0, 0) + dot(s_upper, d_lower, 0, 0) + dot(s_lower, d_upper, 0, 0)


def return_kernel(k_hbm, v_hbm, dk_hbm, dv_hbm, gain_a, gain_b, _, k_ref, v_ref, dk_ref, dv_ref, gain_ref, sems):
    v_half = v_hbm.at[:, pl.ds(0, v_ref.shape[1])]
    copies = fetch(((k_hbm, k_ref), (v_half, v_ref), (dk_hbm, dk_ref), (dv_hbm, dv_ref)), sems)
    gain_ref[...] = gain_a[...] + gain_b[...]
    for copy in copies:
        copy.wait()


def last_kernel(scale, k_ref, v_near, v_hbm, state_ref, dk_in, dv_in, dk_hbm, dv_hbm, v_far, dk_ref, dv_ref, sems):
    wide = v_near.shape[1]
    heads = k_ref.shape[1] // DH
    half = heads // 2
    v_copy = pltpu.make_async_copy(v_hbm.at[:, pl.ds(wide, wide)], v_far, sems.at[4])
    v_copy.start()
    copies = []

    def store(src, dst, part):
        at = pl.ds(part * wide, wide)
        copies.append(pltpu.make_async_copy(src.at[:, at], dst.at[:, at], sems.at[len(copies)]))
        copies[-1].start()

    states = []
    for head in range(heads):
        at = columns(head)
        upper, lower = halves(state_ref[at, :])
        states.append((upper, lower))
        k = k_ref[:, at]
        dv = dv_in[:, at] + dot(jnp.concatenate([k, k], 1), jnp.concatenate([upper, lower], 0))
        dv_ref[:, at] = (scale * dv).astype(dv_ref.dtype)
        if head % half == half - 1:
            store(dv_ref, dv_hbm, head // half)
    for head in range(heads):
        at = columns(head)
        if head == half:
            v_copy.wait()
        v = v_near[:, at] if head < half else v_far[:, columns(head - half)]
        dk = dk_in[:, at] + dot(jnp.concatenate([v, v], 1), jnp.concatenate(states[head], 1), 1, 1)
        dk_ref[:, at] = (scale * dk).astype(dk_ref.dtype)
        if head % half == half - 1:
            store(dk_ref, dk_hbm, head // half)
    for copy in copies:
        copy.wait()


def body(queries, keys, values, gain, grad_out):
    _, tokens, wide = queries.shape
    q, k, v, dy = (a.reshape(tokens, wide) for a in (queries, keys, values, grad_out))
    gain = gain.reshape(1, wide)
    heads = wide // DH
    ctx, shards = lax.axis_size("ctx"), lax.axis_size("heads")
    width = float(shards * wide)
    scale = DH ** (-0.5)
    rows = wide // ctx
    per = 2 * tokens * DH * DH * heads
    all_tok = (tokens, wide)
    exchange = functools.partial(lax.all_to_all, axis_name="ctx", split_axis=0, concat_axis=0, tiled=True)

    inputs = [(a, "hbm") for a in (q, k, v, dy, gain)]
    near = [(all_tok, F32, "vmem"), (all_tok, BF16, "vmem"), (all_tok, BF16, "vmem"), ((1, wide), F32, "vmem")]
    inner = [pltpu.VMEM(all_tok, BF16), pltpu.VMEM(all_tok, BF16), pltpu.SemaphoreType.DMA((5,))]
    local, *held = call(states_kernel, "key_value_states", inputs, [((wide, DH), F32, "")] + near, 4 * per, inner)
    parts = exchange(local).reshape(ctx, rows, DH)
    within, q_near, dy_near, gain_near = call(
        within_kernel,
        "within_block",
        inputs + [(a, "vmem") for a in held],
        near,
        6 * per,
        inner,
        {len(inputs) + i: i for i in range(len(held))},
    )
    scan_room = [pltpu.VMEM((ctx, rows, DH), F32), pltpu.SemaphoreType.DMA((4,))]
    (before,) = call(
        prefix_kernel, "prefix", [(parts, "")], [((ctx, rows, DH), F32, "hbm raw")], wide * DH, scan_room
    )
    prefix = exchange(before.reshape(wide, DH))
    attn, sums = call(
        functools.partial(attend_kernel, scale),
        "attend",
        [(q_near, "vmem"), (within, "vmem"), (prefix, ""), (gain_near, "vmem"), (dy_near, "vmem")],
        [(all_tok, F32, "vmem"), ((shards, 2 * tokens // DH, DH), F32, "")],
        2 * per,
    )
    sums = lax.all_to_all(sums, "heads", 0, 0, tiled=True)
    grad_local, factors = call(
        functools.partial(grad_state_kernel, width),
        "grad_states",
        [(sums, ""), (q_near, "vmem"), (attn, "vmem"), (gain_near, "vmem"), (dy_near, "vmem")],
        [((ctx, rows + heads, DH), F32, "hbm raw"), ((2, tokens, DH), F32, "vmem")],
        2 * per,
        [pltpu.VMEM((ctx, rows + heads, DH), F32), pltpu.SemaphoreType.DMA((heads // 2 + 1,))],
    )
    grad_parts = exchange(grad_local)
    output, d_query, dk_part, dv_part = call(
        functools.partial(backward_kernel, scale),
        "backward_within",
        [(q, "hbm"), (k, "hbm"), (v, "hbm"), (dy, "hbm"), (gain_near, "vmem"), (attn, "vmem"), (prefix, ""), (factors, "vmem")],
        [(all_tok, BF16, "hbm"), (all_tok, BF16, "hbm"), (all_tok, F32, "hbm"), (all_tok, F32, "hbm")],
        22 * per,
        [pltpu.VMEM(all_tok, BF16)] * 4 + [pltpu.SemaphoreType.DMA((4,))],
    )
    total_rows = lax.axis_size("dp") * ctx * tokens
    after, gain_sum = call(
        functools.partial(suffix_kernel, 1.0 / math.sqrt(total_rows)),
        "suffix",
        [(grad_parts, ""), (dv_part, "hbm")],
        [((ctx, rows, DH), F32, "hbm raw"), ((heads, DH), F32, "")],
        wide * DH,
        scan_room,
    )
    suffix = exchange(after.reshape(wide, DH))
    gain_other = lax.ppermute(gain_sum, "dp", [(i, lax.axis_size("dp") - 1 - i) for i in range(lax.axis_size("dp"))])
    k_near, v_near, dk_near, dv_near, grad_gain = call(
        return_kernel,
        "return_operands",
        [(k, "hbm"), (v, "hbm"), (dk_part, "hbm"), (dv_part, "hbm"), (gain_sum, ""), (gain_other, ""), (after, "hbm")],
        [(all_tok, BF16, "vmem"), ((tokens, wide // 2), BF16, "vmem"), (all_tok, F32, "vmem"), (all_tok, F32, "vmem"), ((heads, DH), F32, "hbm")],
        wide * DH,
        [pltpu.SemaphoreType.DMA((4,))],
    )
    d_key, d_value = call(
        functools.partial(last_kernel, scale),
        "key_value_gradients",
        [(k_near, "vmem"), (v_near, "vmem"), (v, "hbm"), (suffix, ""), (dk_near, "vmem"), (dv_near, "vmem")],
        [(all_tok, BF16, "hbm raw"), (all_tok, BF16, "hbm raw")],
        4 * per,
        [pltpu.VMEM((tokens, wide // 2), BF16)] + [pltpu.VMEM(all_tok, BF16)] * 2 + [pltpu.SemaphoreType.DMA((5,))],
    )
    return (*(a[None] for a in (output, d_query, d_key, d_value)), grad_gain.reshape(wide))


def solution(mesh):
    placed = P("dp", "ctx", "heads")
    return jax.shard_map(
        body,
        mesh=mesh,
        in_specs=(placed, placed, placed, P("heads"), placed),
        out_specs=(placed, placed, placed, placed, P("heads")),
        check_vma=False,
    )
```

```python
import functools
import math

import jax
import jax.numpy as jnp
from jax import lax
from jax.experimental import pallas as pl
from jax.experimental.pallas import tpu as pltpu
from jax.sharding import PartitionSpec as P

DH = 128
epsilon = 1e-05
F32 = jnp.float32
BF16 = jnp.bfloat16
VMEM_GRANT = 16 * 1024 * 1024
SUFFIX_OUT = "hbm"


def halves(x):
    upper = x.astype(BF16)
    return upper, (x - upper.astype(F32)).astype(BF16)


def dot(a, b, ca=1, cb=0):
    return lax.dot_general(a, b, (((ca,), (cb,)), ((), ())), preferred_element_type=F32)


def columns(head):
    return slice(head * DH, (head + 1) * DH)


def causal(x):
    row = lax.broadcasted_iota(jnp.int32, x.shape, 0)
    column = lax.broadcasted_iota(jnp.int32, x.shape, 1)
    return jnp.where(row >= column, x, 0.0)


def call(kernel, name, ins, outs, flops, scratch=(), aliases=None):
    spaces = {"vmem": pltpu.VMEM, "hbm": pltpu.HBM}
    arrays = [pltpu.with_memory_space_constraint(a, spaces[w]) if w else a for a, w in ins]
    moved = sum(a.size * a.dtype.itemsize for a, _ in ins)
    moved += sum(math.prod(shape) * jnp.dtype(kind).itemsize for shape, kind, _ in outs)

    def spec(where):
        return pl.BlockSpec(memory_space=pl.ANY if where == "hbm" else pltpu.VMEM)

    return pl.pallas_call(
        kernel,
        name=name,
        in_specs=[spec(w) for _, w in ins],
        out_specs=[spec("hbm" if w == "hbm raw" else "") for _, _, w in outs],
        out_shape=[
            spaces["hbm" if w == "hbm raw" else w](shape, kind) if w else jax.ShapeDtypeStruct(shape, kind)
            for shape, kind, w in outs
        ],
        scratch_shapes=scratch,
        input_output_aliases=aliases or {},
        cost_estimate=pl.CostEstimate(flops=flops, bytes_accessed=moved, transcendentals=0),
        compiler_params=pltpu.CompilerParams(vmem_limit_bytes=VMEM_GRANT),
    )(*arrays)


def fetch(pairs, sems):
    copies = [pltpu.make_async_copy(src, dst, sems.at[i]) for i, (src, dst) in enumerate(pairs)]
    for copy in copies:
        copy.start()
    return copies


def attend_within(q_ref, k_ref, v_ref, within_ref):
    def one(head, _):
        at = pl.ds(pl.multiple_of(head * DH, DH), DH)
        upper, lower = halves(causal(dot(q_ref[:, at], k_ref[:, at], 1, 1)))
        v = v_ref[:, at]
        within_ref[:, at] = dot(upper, v) + dot(lower, v)
        return 0

    lax.fori_loop(0, q_ref.shape[1] // DH, one, 0)


def states_kernel(q_hbm, k_hbm, v_hbm, dy_hbm, gain_hbm, state_ref, within_ref, q_ref, dy_ref, gain_ref, k_ref, v_ref, sems):
    for copy in fetch(((k_hbm, k_ref), (v_hbm, v_ref)), sems):
        copy.wait()
    for head in range(k_ref.shape[1] // DH):
        at = columns(head)
        state_ref[at, :] = dot(k_ref[:, at], v_ref[:, at], 0, 0)

    @pl.when(lax.axis_index("dp") == 0)
    def _():
        for copy in fetch(((q_hbm, q_ref), (dy_hbm, dy_ref), (gain_hbm, gain_ref)), sems):
            copy.wait()
        attend_within(q_ref, k_ref, v_ref, within_ref)


def within_kernel(q_hbm, k_hbm, v_hbm, dy_hbm, gain_hbm, *refs):
    within_ref, q_ref, dy_ref, gain_ref, k_ref, v_ref, sems = refs[4:]

    @pl.when(lax.axis_index("dp") != 0)
    def _():
        copies = fetch(
            ((q_hbm, q_ref), (k_hbm, k_ref), (v_hbm, v_ref), (dy_hbm, dy_ref), (gain_hbm, gain_ref)), sems
        )
        for copy in copies:
            copy.wait()
        attend_within(q_ref, k_ref, v_ref, within_ref)


def scan(part_ref, out_ref, out_hbm, sems, reverse):
    count, rows = part_ref.shape[0], out_ref.shape[1]
    group = count // sems.shape[0]
    total = jnp.zeros(out_ref.shape[1:], F32)
    copies = []
    for i in range(count):
        place = count - 1 - i if reverse else i
        out_ref[place] = total
        total = total + part_ref[place, :rows]
        if i % group == group - 1:
            at = pl.ds(place if reverse else place + 1 - group, group)
            copies.append(pltpu.make_async_copy(out_ref.at[at], out_hbm.at[at], sems.at[len(copies)]))
            copies[-1].start()
    return copies


def prefix_kernel(part_ref, out_hbm, out_ref, sems):
    for copy in scan(part_ref, out_ref, out_hbm, sems, False):
        copy.wait()


def suffix_kernel(gain_scale, part_ref, _, out_hbm, gain_ref, out_ref, sems):
    copies = scan(part_ref, out_ref, out_hbm, sems, True)
    rows = out_ref.shape[1]
    gain = jnp.zeros(gain_ref.shape, F32)
    for i in range(part_ref.shape[0]):
        gain = gain + part_ref[i, rows:]
    gain_ref[...] = gain_scale * gain
    for copy in copies:
        copy.wait()


def attend_kernel(scale, q_ref, within_ref, state_ref, gain_ref, dy_ref, attn_ref, sums_ref):
    tokens = q_ref.shape[0]
    squares = jnp.zeros((tokens, DH), F32)
    inner = jnp.zeros((tokens, DH), F32)
    for head in range(q_ref.shape[1] // DH):
        at = columns(head)
        q = q_ref[:, at]
        upper, lower = halves(state_ref[at, :])
        before = dot(jnp.concatenate([q, q], 1), jnp.concatenate([upper, lower], 0))
        attn = scale * (within_ref[:, at] + before)
        attn_ref[:, at] = attn
        squares += attn * attn
        inner += (gain_ref[:, at] * dy_ref[:, at].astype(F32)) * attn
    rows = []
    for total in (squares, inner):
        line = jnp.sum(total.T, axis=0, keepdims=True)
        rows += [line[:, i : i + DH] for i in range(0, tokens, DH)]
    sums = jnp.concatenate(rows, 0)
    for i in range(sums_ref.shape[0]):
        sums_ref[i] = sums


def token_factors(sums_ref, width):
    sums = sums_ref[0]
    for i in range(1, sums_ref.shape[0]):
        sums = sums + sums_ref[i]
    count = sums.shape[0] // 2
    inverse = 1.0 / jnp.sqrt(sums[:count] / width + epsilon)
    other = sums[count:] * (inverse * inverse * inverse) / width
    both = jnp.concatenate([inverse, other, jnp.zeros((8 - 2 * count, DH), F32)], 0).T

    def spread(first):
        return jnp.concatenate([jnp.broadcast_to(both[:, i : i + 1], (DH, DH)) for i in range(first, first + count)], 0)

    return spread(0), spread(count)


def grad_state_kernel(width, sums_ref, q_ref, attn_ref, gain_ref, dy_ref, state_hbm, factor_ref, state_ref, sems):
    inverse, other = token_factors(sums_ref, width)
    factor_ref[0] = inverse
    factor_ref[1] = other
    heads = q_ref.shape[1] // DH
    per_head = state_ref.shape[0] // heads
    rows = DH // per_head
    copies = []

    def send(slices, part):
        at = (slices, part)
        copies.append(pltpu.make_async_copy(state_ref.at[at], state_hbm.at[at], sems.at[len(copies)]))
        copies[-1].start()

    weights = []
    for head in range(heads):
        at = columns(head)
        weights.append(jnp.sum(dy_ref[:, at].astype(F32) * (attn_ref[:, at] * inverse), axis=0, keepdims=True))
    weights = jnp.concatenate(weights, 0)
    for i in range(state_ref.shape[0]):
        state_ref[i, rows:, :] = weights
    send(pl.ds(0, state_ref.shape[0]), pl.ds(rows, heads))
    for head in range(heads):
        at = columns(head)
        d_attn = (gain_ref[:, at] * dy_ref[:, at].astype(F32)) * inverse - attn_ref[:, at] * other
        upper, lower = halves(d_attn)
        q = q_ref[:, at]
        state = dot(q, upper, 0, 0) + dot(q, lower, 0, 0)
        state_ref[head * per_head : (head + 1) * per_head, :rows, :] = state.reshape(per_head, rows, DH)
        if head % 2:
            send(pl.ds((head - 1) * per_head, 2 * per_head), pl.ds(0, rows))
    for copy in copies:
        copy.wait()


def backward_kernel(scale, q_hbm, k_hbm, v_hbm, dy_hbm, gain_ref, attn_ref, state_ref, factor_ref, out_ref, dq_ref, dk_ref, dv_ref, k_ref, v_ref, q_ref, dy_ref, sems):
    copies = fetch(((q_hbm, q_ref), (k_hbm, k_ref), (v_hbm, v_ref), (dy_hbm, dy_ref)), sems)
    for copy in copies:
        copy.wait()
    inverse = factor_ref[0]
    other = factor_ref[1]
    for head in range(q_ref.shape[1] // DH):
        at = columns(head)
        q, k, v = q_ref[:, at], k_ref[:, at], v_ref[:, at]
        gain = gain_ref[:, at]
        attn = attn_ref[:, at]
        out_ref[:, at] = (gain * (attn * inverse)).astype(out_ref.dtype)
        d_attn = (gain * dy_ref[:, at].astype(F32)) * inverse - attn * other
        d_upper, d_lower = halves(d_attn)
        d_both = jnp.concatenate([d_upper, d_lower], 1)
        s_upper, s_lower = halves(causal(dot(q, k, 1, 1)))
        ds_upper, ds_lower = halves(causal(dot(d_both, jnp.concatenate([v, v], 1), 1, 1)))
        p_upper, p_lower = halves(state_ref[at, :])
        dq = dot(ds_upper, k) + dot(ds_lower, k)
        dq += dot(d_both, jnp.concatenate([p_upper, p_upper], 1), 1, 1)
        dq += dot(d_upper, p_lower, 1, 1)
        dq_ref[:, at] = (scale * dq).astype(dq_ref.dtype)
        dk_ref[:, at] = dot(ds_upper, q, 0, 0) + dot(ds_lower, q, 0, 0)
        dv_ref[:, at] = dot(s_upper, d_upper, 0, 0) + dot(s_upper, d_lower, 0, 0) + dot(s_lower, d_upper, 0, 0)


def return_kernel(k_hbm, v_hbm, dk_hbm, dv_hbm, gain_a, gain_b, _, k_ref, v_ref, dk_ref, dv_ref, gain_ref, sems):
    dk_first = dk_hbm.at[:, pl.ds(0, dk_ref.shape[1])]
    copies = fetch(((k_hbm, k_ref), (v_hbm, v_ref), (dk_first, dk_ref), (dv_hbm, dv_ref)), sems)
    gain_ref[...] = gain_a[...] + gain_b[...]
    for copy in copies:
        copy.wait()


def last_kernel(scale, k_ref, v_ref, state_ref, dk_near, dk_part, dv_in, dk_hbm, dv_hbm, dk_far, dk_ref, dv_ref, sems):
    heads = k_ref.shape[1] // DH
    near = dk_near.shape[1] // DH
    half = heads // 2
    far_copy = pltpu.make_async_copy(dk_part.at[:, pl.ds(near * DH, (heads - near) * DH)], dk_far, sems.at[4])
    far_copy.start()
    copies = []

    def store(src, dst, part):
        at = pl.ds(part * half * DH, half * DH)
        copies.append(pltpu.make_async_copy(src.at[:, at], dst.at[:, at], sems.at[len(copies)]))
        copies[-1].start()

    states = []
    for head in range(heads):
        at = columns(head)
        upper, lower = halves(state_ref[at, :])
        states.append((upper, lower))
        k = k_ref[:, at]
        dv = dv_in[:, at] + dot(jnp.concatenate([k, k], 1), jnp.concatenate([upper, lower], 0))
        dv_ref[:, at] = (scale * dv).astype(dv_ref.dtype)
        if head % half == half - 1:
            store(dv_ref, dv_hbm, head // half)
    for head in range(heads):
        at = columns(head)
        if head == near:
            far_copy.wait()
        v = v_ref[:, at]
        dk = dk_near[:, at] if head < near else dk_far[:, columns(head - near)]
        dk = dk + dot(jnp.concatenate([v, v], 1), jnp.concatenate(states[head], 1), 1, 1)
        dk_ref[:, at] = (scale * dk).astype(dk_ref.dtype)
        if head % half == half - 1:
            store(dk_ref, dk_hbm, head // half)
    for copy in copies:
        copy.wait()


def body(queries, keys, values, gain, grad_out):
    _, tokens, wide = queries.shape
    q, k, v, dy = (a.reshape(tokens, wide) for a in (queries, keys, values, grad_out))
    gain = gain.reshape(1, wide)
    heads = wide // DH
    ctx, shards = lax.axis_size("ctx"), lax.axis_size("heads")
    width = float(shards * wide)
    scale = DH ** (-0.5)
    rows = wide // ctx
    per = 2 * tokens * DH * DH * heads
    all_tok = (tokens, wide)
    near_tok = (tokens, wide - wide // 4)
    exchange = functools.partial(lax.all_to_all, axis_name="ctx", split_axis=0, concat_axis=0, tiled=True)

    inputs = [(a, "hbm") for a in (q, k, v, dy, gain)]
    near = [(all_tok, F32, "vmem"), (all_tok, BF16, "vmem"), (all_tok, BF16, "vmem"), ((1, wide), F32, "vmem")]
    inner = [pltpu.VMEM(all_tok, BF16), pltpu.VMEM(all_tok, BF16), pltpu.SemaphoreType.DMA((5,))]
    local, *held = call(states_kernel, "key_value_states", inputs, [((wide, DH), F32, "")] + near, 4 * per, inner)
    parts = exchange(local).reshape(ctx, rows, DH)
    within, q_near, dy_near, gain_near = call(
        within_kernel,
        "within_block",
        inputs + [(a, "vmem") for a in held],
        near,
        6 * per,
        inner,
        {len(inputs) + i: i for i in range(len(held))},
    )
    scan_room = [pltpu.VMEM((ctx, rows, DH), F32), pltpu.SemaphoreType.DMA((4,))]
    (before,) = call(
        prefix_kernel, "prefix", [(parts, "")], [((ctx, rows, DH), F32, "hbm raw")], wide * DH, scan_room
    )
    prefix = exchange(before.reshape(wide, DH))
    attn, sums = call(
        functools.partial(attend_kernel, scale),
        "attend",
        [(q_near, "vmem"), (within, "vmem"), (prefix, ""), (gain_near, "vmem"), (dy_near, "vmem")],
        [(all_tok, F32, "vmem"), ((shards, 2 * tokens // DH, DH), F32, "")],
        2 * per,
    )
    sums = lax.all_to_all(sums, "heads", 0, 0, tiled=True)
    grad_local, factors = call(
        functools.partial(grad_state_kernel, width),
        "grad_states",
        [(sums, ""), (q_near, "vmem"), (attn, "vmem"), (gain_near, "vmem"), (dy_near, "vmem")],
        [((ctx, rows + heads, DH), F32, "hbm raw"), ((2, tokens, DH), F32, "vmem")],
        2 * per,
        [pltpu.VMEM((ctx, rows + heads, DH), F32), pltpu.SemaphoreType.DMA((heads // 2 + 1,))],
    )
    grad_parts = exchange(grad_local)
    output, d_query, dk_part, dv_part = call(
        functools.partial(backward_kernel, scale),
        "backward_within",
        [(q, "hbm"), (k, "hbm"), (v, "hbm"), (dy, "hbm"), (gain_near, "vmem"), (attn, "vmem"), (prefix, ""), (factors, "vmem")],
        [(all_tok, BF16, "hbm"), (all_tok, BF16, "hbm"), (all_tok, F32, "hbm"), (all_tok, F32, "hbm")],
        22 * per,
        [pltpu.VMEM(all_tok, BF16)] * 4 + [pltpu.SemaphoreType.DMA((4,))],
    )
    total_rows = lax.axis_size("dp") * ctx * tokens
    after, gain_sum = call(
        functools.partial(suffix_kernel, 1.0 / math.sqrt(total_rows)),
        "suffix",
        [(grad_parts, ""), (dv_part, "hbm")],
        [((ctx, rows, DH), F32, "hbm raw"), ((heads, DH), F32, "")],
        wide * DH,
        scan_room,
    )
    suffix = exchange(after.reshape(wide, DH))
    gain_other = lax.ppermute(gain_sum, "dp", [(i, lax.axis_size("dp") - 1 - i) for i in range(lax.axis_size("dp"))])
    k_near, v_near, dk_near, dv_near, grad_gain = call(
        return_kernel,
        "return_operands",
        [(k, "hbm"), (v, "hbm"), (dk_part, "hbm"), (dv_part, "hbm"), (gain_sum, ""), (gain_other, ""), (after, "hbm")],
        [(all_tok, BF16, "vmem"), (all_tok, BF16, "vmem"), (near_tok, F32, "vmem"), (all_tok, F32, "vmem"), ((heads, DH), F32, "hbm")],
        wide * DH,
        [pltpu.SemaphoreType.DMA((4,))],
    )
    d_key, d_value = call(
        functools.partial(last_kernel, scale),
        "key_value_gradients",
        [(k_near, "vmem"), (v_near, "vmem"), (suffix, ""), (dk_near, "vmem"), (dk_part, "hbm"), (dv_near, "vmem")],
        [(all_tok, BF16, "hbm raw"), (all_tok, BF16, "hbm raw")],
        4 * per,
        [pltpu.VMEM((tokens, wide // 4), F32)] + [pltpu.VMEM(all_tok, BF16)] * 2 + [pltpu.SemaphoreType.DMA((5,))],
    )
    return (*(a[None] for a in (output, d_query, d_key, d_value)), grad_gain.reshape(wide))


def solution(mesh):
    placed = P("dp", "ctx", "heads")
    return jax.shard_map(
        body,
        mesh=mesh,
        in_specs=(placed, placed, placed, P("heads"), placed),
        out_specs=(placed, placed, placed, placed, P("heads")),
        check_vma=False,
    )
```

```python
import functools
import math

import jax
import jax.numpy as jnp
from jax import lax
from jax.experimental import pallas as pl
from jax.experimental.pallas import tpu as pltpu
from jax.sharding import PartitionSpec as P

DH = 128
epsilon = 1e-05
F32 = jnp.float32
BF16 = jnp.bfloat16
VMEM_GRANT = 16 * 1024 * 1024
FIRST = 7
FIRST_HEADS = 4
SUFFIX_OUT = "hbm"


def halves(x):
    upper = x.astype(BF16)
    return upper, (x - upper.astype(F32)).astype(BF16)


def dot(a, b, ca=1, cb=0):
    return lax.dot_general(a, b, (((ca,), (cb,)), ((), ())), preferred_element_type=F32)


def columns(head):
    return slice(head * DH, (head + 1) * DH)


def causal(x):
    row = lax.broadcasted_iota(jnp.int32, x.shape, 0)
    column = lax.broadcasted_iota(jnp.int32, x.shape, 1)
    return jnp.where(row >= column, x, 0.0)


def call(kernel, name, ins, outs, flops, scratch=(), aliases=None):
    spaces = {"vmem": pltpu.VMEM, "hbm": pltpu.HBM}
    arrays = [pltpu.with_memory_space_constraint(a, spaces[w]) if w else a for a, w in ins]
    moved = sum(a.size * a.dtype.itemsize for a, _ in ins)
    moved += sum(math.prod(shape) * jnp.dtype(kind).itemsize for shape, kind, _ in outs)

    def spec(where):
        return pl.BlockSpec(memory_space=pl.ANY if where == "hbm" else pltpu.VMEM)

    return pl.pallas_call(
        kernel,
        name=name,
        in_specs=[spec(w) for _, w in ins],
        out_specs=[spec("hbm" if w == "hbm raw" else "") for _, _, w in outs],
        out_shape=[
            spaces["hbm" if w == "hbm raw" else w](shape, kind) if w else jax.ShapeDtypeStruct(shape, kind)
            for shape, kind, w in outs
        ],
        scratch_shapes=scratch,
        input_output_aliases=aliases or {},
        cost_estimate=pl.CostEstimate(flops=flops, bytes_accessed=moved, transcendentals=0),
        compiler_params=pltpu.CompilerParams(vmem_limit_bytes=VMEM_GRANT),
    )(*arrays)


def fetch(pairs, sems):
    copies = [pltpu.make_async_copy(src, dst, sems.at[i]) for i, (src, dst) in enumerate(pairs)]
    for copy in copies:
        copy.start()
    return copies


def attend_within(q_ref, k_ref, v_ref, within_ref):
    def one(head, _):
        at = pl.ds(pl.multiple_of(head * DH, DH), DH)
        upper, lower = halves(causal(dot(q_ref[:, at], k_ref[:, at], 1, 1)))
        v = v_ref[:, at]
        within_ref[:, at] = dot(upper, v) + dot(lower, v)
        return 0

    lax.fori_loop(0, q_ref.shape[1] // DH, one, 0)


def states_kernel(q_hbm, k_hbm, v_hbm, dy_hbm, gain_hbm, state_ref, within_ref, q_ref, dy_ref, gain_ref, k_ref, v_ref, sems):
    for copy in fetch(((k_hbm, k_ref), (v_hbm, v_ref)), sems):
        copy.wait()
    for head in range(k_ref.shape[1] // DH):
        at = columns(head)
        state_ref[at, :] = dot(k_ref[:, at], v_ref[:, at], 0, 0)

    @pl.when(lax.axis_index("dp") == 0)
    def _():
        for copy in fetch(((q_hbm, q_ref), (dy_hbm, dy_ref), (gain_hbm, gain_ref)), sems):
            copy.wait()
        attend_within(q_ref, k_ref, v_ref, within_ref)


def within_kernel(q_hbm, k_hbm, v_hbm, dy_hbm, gain_hbm, *refs):
    within_ref, q_ref, dy_ref, gain_ref, k_ref, v_ref, sems = refs[4:]

    @pl.when(lax.axis_index("dp") != 0)
    def _():
        copies = fetch(
            ((q_hbm, q_ref), (k_hbm, k_ref), (v_hbm, v_ref), (dy_hbm, dy_ref), (gain_hbm, gain_ref)), sems
        )
        for copy in copies:
            copy.wait()
        attend_within(q_ref, k_ref, v_ref, within_ref)


def scan(part_ref, out_ref, out_hbm, sems, reverse):
    count, rows = part_ref.shape[0], out_ref.shape[1]
    group = count // sems.shape[0]
    total = jnp.zeros(out_ref.shape[1:], F32)
    copies = []
    left = [group] * sems.shape[0]
    for i in range(count):
        place = ((count - 1 - i if reverse else i) - FIRST) % count
        out_ref[place] = total
        total = total + part_ref[place, :rows]
        part = place // group
        left[part] -= 1
        if not left[part]:
            at = pl.ds(part * group, group)
            copies.append(pltpu.make_async_copy(out_ref.at[at], out_hbm.at[at], sems.at[len(copies)]))
            copies[-1].start()
    return copies


def prefix_kernel(part_ref, out_hbm, out_ref, sems):
    for copy in scan(part_ref, out_ref, out_hbm, sems, False):
        copy.wait()


def suffix_kernel(gain_scale, part_ref, _, out_hbm, gain_ref, out_ref, sems):
    copies = scan(part_ref, out_ref, out_hbm, sems, True)
    rows = out_ref.shape[1]
    gain = jnp.zeros(gain_ref.shape, F32)
    for i in range(part_ref.shape[0]):
        gain = gain + part_ref[i, rows:]
    gain_ref[...] = gain_scale * gain
    for copy in copies:
        copy.wait()


def attend_kernel(scale, q_ref, within_ref, state_ref, gain_ref, dy_ref, attn_ref, sums_ref):
    tokens = q_ref.shape[0]
    squares = jnp.zeros((tokens, DH), F32)
    inner = jnp.zeros((tokens, DH), F32)
    for head in range(q_ref.shape[1] // DH):
        at = columns(head)
        q = q_ref[:, at]
        upper, lower = halves(state_ref[at, :])
        before = dot(jnp.concatenate([q, q], 1), jnp.concatenate([upper, lower], 0))
        attn = scale * (within_ref[:, at] + before)
        attn_ref[:, at] = attn
        squares += attn * attn
        inner += (gain_ref[:, at] * dy_ref[:, at].astype(F32)) * attn
    rows = []
    for total in (squares, inner):
        line = jnp.sum(total.T, axis=0, keepdims=True)
        rows += [line[:, i : i + DH] for i in range(0, tokens, DH)]
    sums = jnp.concatenate(rows, 0)
    for i in range(sums_ref.shape[0]):
        sums_ref[i] = sums


def token_factors(sums_ref, width):
    sums = sums_ref[0]
    for i in range(1, sums_ref.shape[0]):
        sums = sums + sums_ref[i]
    count = sums.shape[0] // 2
    inverse = 1.0 / jnp.sqrt(sums[:count] / width + epsilon)
    other = sums[count:] * (inverse * inverse * inverse) / width
    both = jnp.concatenate([inverse, other, jnp.zeros((8 - 2 * count, DH), F32)], 0).T

    def spread(first):
        return jnp.concatenate([jnp.broadcast_to(both[:, i : i + 1], (DH, DH)) for i in range(first, first + count)], 0)

    return spread(0), spread(count)


def grad_state_kernel(width, sums_ref, q_ref, attn_ref, gain_ref, dy_ref, state_hbm, factor_ref, state_ref, sems):
    inverse, other = token_factors(sums_ref, width)
    factor_ref[0] = inverse
    factor_ref[1] = other
    heads = q_ref.shape[1] // DH
    per_head = state_ref.shape[0] // heads
    rows = DH // per_head
    copies = []

    def send(slices, part):
        at = (slices, part)
        copies.append(pltpu.make_async_copy(state_ref.at[at], state_hbm.at[at], sems.at[len(copies)]))
        copies[-1].start()

    weights = []
    for head in range(heads):
        at = columns(head)
        weights.append(jnp.sum(dy_ref[:, at].astype(F32) * (attn_ref[:, at] * inverse), axis=0, keepdims=True))
    weights = jnp.concatenate(weights, 0)
    for i in range(state_ref.shape[0]):
        state_ref[i, rows:, :] = weights
    send(pl.ds(0, state_ref.shape[0]), pl.ds(rows, heads))
    for head in range(heads):
        at = columns(head)
        d_attn = (gain_ref[:, at] * dy_ref[:, at].astype(F32)) * inverse - attn_ref[:, at] * other
        upper, lower = halves(d_attn)
        q = q_ref[:, at]
        both = dot(q, jnp.concatenate([upper, lower], 1), 0, 0)
        state = both[:, :DH] + both[:, DH:]
        state_ref[head * per_head : (head + 1) * per_head, :rows, :] = state.reshape(per_head, rows, DH)
        if head % 2:
            send(pl.ds((head - 1) * per_head, 2 * per_head), pl.ds(0, rows))
    for copy in copies:
        copy.wait()


def backward_kernel(scale, q_hbm, k_hbm, v_hbm, dy_hbm, gain_ref, attn_ref, state_ref, factor_ref, out_ref, dq_ref, dk_ref, dv_ref, k_ref, v_ref, q_ref, dy_ref, sems):
    copies = fetch(((q_hbm, q_ref), (k_hbm, k_ref), (v_hbm, v_ref), (dy_hbm, dy_ref)), sems)
    for copy in copies:
        copy.wait()
    inverse = factor_ref[0]
    other = factor_ref[1]
    for head in range(q_ref.shape[1] // DH):
        at = columns(head)
        q, k, v = q_ref[:, at], k_ref[:, at], v_ref[:, at]
        gain = gain_ref[:, at]
        attn = attn_ref[:, at]
        out_ref[:, at] = (gain * (attn * inverse)).astype(out_ref.dtype)
        d_attn = (gain * dy_ref[:, at].astype(F32)) * inverse - attn * other
        d_upper, d_lower = halves(d_attn)
        d_both = jnp.concatenate([d_upper, d_lower], 1)
        s_upper, s_lower = halves(causal(dot(q, k, 1, 1)))
        ds_upper, ds_lower = halves(causal(dot(d_both, jnp.concatenate([v, v], 1), 1, 1)))
        p_upper, p_lower = halves(state_ref[at, :])
        dq = dot(ds_upper, k) + dot(ds_lower, k)
        dq += dot(d_both, jnp.concatenate([p_upper, p_upper], 1), 1, 1)
        dq += dot(d_upper, p_lower, 1, 1)
        dq_ref[:, at] = (scale * dq).astype(dq_ref.dtype)
        dk_ref[:, at] = dot(ds_upper, q, 0, 0) + dot(ds_lower, q, 0, 0)
        dv_ref[:, at] = dot(s_upper, d_upper, 0, 0) + dot(s_upper, d_lower, 0, 0) + dot(s_lower, d_upper, 0, 0)


def return_kernel(k_hbm, v_hbm, dk_hbm, dv_hbm, gain_a, gain_b, _, k_ref, v_ref, dk_ref, dv_ref, gain_ref, sems):
    dk_first = dk_hbm.at[:, pl.ds(0, dk_ref.shape[1])]
    copies = fetch(((k_hbm, k_ref), (v_hbm, v_ref), (dk_first, dk_ref), (dv_hbm, dv_ref)), sems)
    gain_ref[...] = gain_a[...] + gain_b[...]
    for copy in copies:
        copy.wait()


def last_kernel(scale, k_ref, v_ref, state_ref, dk_near, dk_part, dv_in, dk_hbm, dv_hbm, dk_far, dk_ref, dv_ref, sems):
    heads = k_ref.shape[1] // DH
    near = dk_near.shape[1] // DH
    half = heads // 2
    far_copy = pltpu.make_async_copy(dk_part.at[:, pl.ds(near * DH, (heads - near) * DH)], dk_far, sems.at[4])
    far_copy.start()
    copies = []

    def store(src, dst, part):
        at = pl.ds(part * half * DH, half * DH)
        copies.append(pltpu.make_async_copy(src.at[:, at], dst.at[:, at], sems.at[len(copies)]))
        copies[-1].start()

    states = []
    for head in range(heads):
        at = columns(head)
        upper, lower = halves(state_ref[at, :])
        states.append((upper, lower))
        k = k_ref[:, at]
        dv = dv_in[:, at] + dot(jnp.concatenate([k, k], 1), jnp.concatenate([upper, lower], 0))
        dv_ref[:, at] = (scale * dv).astype(dv_ref.dtype)
        if head % half == half - 1:
            store(dv_ref, dv_hbm, head // half)
    for head in range(heads):
        at = columns(head)
        if head == near:
            far_copy.wait()
        v = v_ref[:, at]
        dk = dk_near[:, at] if head < near else dk_far[:, columns(head - near)]
        dk = dk + dot(jnp.concatenate([v, v], 1), jnp.concatenate(states[head], 1), 1, 1)
        dk_ref[:, at] = (scale * dk).astype(dk_ref.dtype)
        if head % half == half - 1:
            store(dk_ref, dk_hbm, head // half)
    for copy in copies:
        copy.wait()


def body(queries, keys, values, gain, grad_out):
    _, tokens, wide = queries.shape
    q, k, v, dy = (a.reshape(tokens, wide) for a in (queries, keys, values, grad_out))
    gain = gain.reshape(1, wide)
    heads = wide // DH
    ctx, shards = lax.axis_size("ctx"), lax.axis_size("heads")
    width = float(shards * wide)
    scale = DH ** (-0.5)
    rows = wide // ctx
    per = 2 * tokens * DH * DH * heads
    all_tok = (tokens, wide)
    near_tok = (tokens, wide - wide // 4)
    exchange = functools.partial(
        lax.all_to_all,
        axis_name="ctx",
        split_axis=0,
        concat_axis=0,
        tiled=True,
        axis_index_groups=[[(FIRST + i) % ctx for i in range(ctx)]],
    )

    inputs = [(a, "hbm") for a in (q, k, v, dy, gain)]
    near = [(all_tok, F32, "vmem"), (all_tok, BF16, "vmem"), (all_tok, BF16, "vmem"), ((1, wide), F32, "vmem")]
    inner = [pltpu.VMEM(all_tok, BF16), pltpu.VMEM(all_tok, BF16), pltpu.SemaphoreType.DMA((5,))]
    local, *held = call(states_kernel, "key_value_states", inputs, [((wide, DH), F32, "")] + near, 4 * per, inner)
    parts = exchange(local).reshape(ctx, rows, DH)
    within, q_near, dy_near, gain_near = call(
        within_kernel,
        "within_block",
        inputs + [(a, "vmem") for a in held],
        near,
        6 * per,
        inner,
        {len(inputs) + i: i for i in range(len(held))},
    )
    scan_room = [pltpu.VMEM((ctx, rows, DH), F32), pltpu.SemaphoreType.DMA((4,))]
    (before,) = call(
        prefix_kernel, "prefix", [(parts, "")], [((ctx, rows, DH), F32, "hbm raw")], wide * DH, scan_room
    )
    prefix = exchange(before.reshape(wide, DH))
    attn, sums = call(
        functools.partial(attend_kernel, scale),
        "attend",
        [(q_near, "vmem"), (within, "vmem"), (prefix, ""), (gain_near, "vmem"), (dy_near, "vmem")],
        [(all_tok, F32, "vmem"), ((shards, 2 * tokens // DH, DH), F32, "")],
        2 * per,
    )
    sums = lax.all_to_all(
        sums,
        "heads",
        0,
        0,
        tiled=True,
        axis_index_groups=[[(FIRST_HEADS + i) % shards for i in range(shards)]],
    )
    grad_local, factors = call(
        functools.partial(grad_state_kernel, width),
        "grad_states",
        [(sums, ""), (q_near, "vmem"), (attn, "vmem"), (gain_near, "vmem"), (dy_near, "vmem")],
        [((ctx, rows + heads, DH), F32, "hbm raw"), ((2, tokens, DH), F32, "vmem")],
        2 * per,
        [pltpu.VMEM((ctx, rows + heads, DH), F32), pltpu.SemaphoreType.DMA((heads // 2 + 1,))],
    )
    grad_parts = exchange(grad_local)
    output, d_query, dk_part, dv_part = call(
        functools.partial(backward_kernel, scale),
        "backward_within",
        [(q, "hbm"), (k, "hbm"), (v, "hbm"), (dy, "hbm"), (gain_near, "vmem"), (attn, "vmem"), (prefix, ""), (factors, "vmem")],
        [(all_tok, BF16, "hbm"), (all_tok, BF16, "hbm"), (all_tok, F32, "hbm"), (all_tok, F32, "hbm")],
        22 * per,
        [pltpu.VMEM(all_tok, BF16)] * 4 + [pltpu.SemaphoreType.DMA((4,))],
    )
    total_rows = lax.axis_size("dp") * ctx * tokens
    after, gain_sum = call(
        functools.partial(suffix_kernel, 1.0 / math.sqrt(total_rows)),
        "suffix",
        [(grad_parts, ""), (dv_part, "hbm")],
        [((ctx, rows, DH), F32, "hbm raw"), ((heads, DH), F32, "")],
        wide * DH,
        scan_room,
    )
    suffix = exchange(after.reshape(wide, DH))
    gain_other = lax.ppermute(gain_sum, "dp", [(i, lax.axis_size("dp") - 1 - i) for i in range(lax.axis_size("dp"))])
    k_near, v_near, dk_near, dv_near, grad_gain = call(
        return_kernel,
        "return_operands",
        [(k, "hbm"), (v, "hbm"), (dk_part, "hbm"), (dv_part, "hbm"), (gain_sum, ""), (gain_other, ""), (after, "hbm")],
        [(all_tok, BF16, "vmem"), (all_tok, BF16, "vmem"), (near_tok, F32, "vmem"), (all_tok, F32, "vmem"), ((heads, DH), F32, "hbm")],
        wide * DH,
        [pltpu.SemaphoreType.DMA((4,))],
    )
    d_key, d_value = call(
        functools.partial(last_kernel, scale),
        "key_value_gradients",
        [(k_near, "vmem"), (v_near, "vmem"), (suffix, ""), (dk_near, "vmem"), (dk_part, "hbm"), (dv_near, "vmem")],
        [(all_tok, BF16, "hbm raw"), (all_tok, BF16, "hbm raw")],
        4 * per,
        [pltpu.VMEM((tokens, wide // 4), F32)] + [pltpu.VMEM(all_tok, BF16)] * 2 + [pltpu.SemaphoreType.DMA((5,))],
    )
    return (*(a[None] for a in (output, d_query, d_key, d_value)), grad_gain.reshape(wide))


def solution(mesh):
    placed = P("dp", "ctx", "heads")
    return jax.shard_map(
        body,
        mesh=mesh,
        in_specs=(placed, placed, placed, P("heads"), placed),
        out_specs=(placed, placed, placed, placed, P("heads")),
        check_vma=False,
    )
```
